256 devices in a mesh: row: 4 (over x), ta: 64 (over z, y, core).
Axes of the slice: x: 4, y: 4, z: 8, core: 2. Of those that a mesh axis runs over, the one named last changes fastest.
Arguments:
- grid: bfloat16 [64, 512, 2048], P('row', 'ta'), may hold values from -6 to 6
- omega: float32 [64, 512], P('row', 'ta'), may hold values from -0.002 to 0.002
- legendre_weights: bfloat16 [512, 512, 256], P('ta', 'row'), may hold values from -1 to 1, as said below
- radial_inverses: float32 [512, 4096], P('row'), may hold values from -1 to 2
Outputs:
- new_spectrum: bfloat16 [512, 512, 256], P('ta', 'row')
The draws below stay inside these ranges and needn't reach their ends.
Inputs may be any that keep to these rules, and one draw needn't show every extreme that they name: legendre_weights[s, k, :] is zero wherever l(k) < m(s).
All inputs are finite; a program needn't handle non-finite values.
Results may differ from the reference program's by a relative error of at most 0.0059.
Values may be sent and summed in bfloat16 or wider, within the bound.
A program may use at most 64 MiB of HBM per device.

```python
import jax
import jax.numpy as jnp
from jax import lax

M = 512
NLAT = 512
NR = 64
N_ROW = 4


def slot_order_drawn(count):
    positions = jnp.arange(count)
    pair_index = positions // 2
    return jnp.where(positions % 2 == 0, pair_index, count - 1 - pair_index)


def degree_order(count, row_count):
    block_size = count // (2 * row_count)
    positions = jnp.arange(count)
    which_block = positions // block_size
    group_index = which_block // 2
    actual_block = jnp.where(which_block % 2 == 0, group_index, 2 * row_count - 1 - group_index)
    return actual_block * block_size + positions % block_size


def draw_legendre_weights(key, part):
    key = jax.random.fold_in(key, 11)
    half_lats = NLAT // 2
    orders = slot_order_drawn(M)
    degrees = degree_order(M, N_ROW)
    alive_mask = (degrees[None, :] >= orders[:, None]).astype(jnp.float32)[:, :, None]
    second_key = jax.random.fold_in(key, 1)
    random_part = jax.random.normal(second_key, (M, M, half_lats))
    return (jnp.clip(random_part * half_lats ** (-0.5), -1.0, 1.0) * alive_mask).astype(jnp.bfloat16)


def draw_radial_inverses(key, part):
    key = jax.random.fold_in(key, 12)
    first_key, second_key = jax.random.split(key)
    diagonal = jax.random.uniform(first_key, (M, NR), minval=1.0, maxval=2.0)
    coupling = jax.random.normal(second_key, (M, NR, NR))
    coupling = jnp.clip(coupling * 0.5 * NR ** (-0.5), -1.0, 1.0)
    identity = jnp.eye(NR, dtype=jnp.float32)
    full = coupling * (1.0 - identity) + diagonal[:, :, None] * identity
    return full.reshape(M, NR * NR)


def level_of(rng, shape, cuts, low, largest):
    level = 1.0
    for position, shards_of in cuts:
        steps = jax.random.uniform(jax.random.fold_in(jax.random.fold_in(rng, 6), position), (shards_of,), jnp.float32, low / len(cuts), largest / len(cuts))
        level = level * jnp.repeat(jnp.exp(steps), shape[position] // shards_of).reshape((-1,) + (1,) * (len(shape) - 1 - position))
    return level


def gaussian(rng, extent, deviation, bound, cuts=(), held_as=jnp.bfloat16):
    result = jax.random.normal(rng, extent, jnp.float32) * deviation
    if len(cuts) > 0:
        result = level_of(rng, extent, cuts, -0.22, 0.18) * result
    return jnp.clip(result, min=-bound, max=bound).astype(held_as)


def setup_inputs(seed: int = 0) -> dict:
    splits = jax.random.split(jax.random.key(seed), 5)
    grid = gaussian(splits[0], (NR, NLAT, M * 4), 1.0, 6.0, ((0, 4), (1, 64)))
    omega = jnp.clip(jax.random.uniform(splits[1], (NR, NLAT), jnp.float32, -0.002, 0.002) * level_of(splits[1], (NR, NLAT), ((0, 4), (1, 64)), -0.4, 0.0), -0.002, 0.002)
    legendre_weights = draw_legendre_weights(jax.random.fold_in(splits[4], 71), 0)
    radial_inverses = draw_radial_inverses(jax.random.fold_in(splits[4], 71), 0)
    return dict(grid=grid, omega=omega, legendre_weights=legendre_weights, radial_inverses=radial_inverses)


def slot_order(count):
    positions = jnp.arange(count)
    pair_index = positions // 2
    return jnp.where(positions % 2 == 0, pair_index, count - 1 - pair_index)


def reference(grid, omega, legendre_weights, radial_inverses):
    half_lats = NLAT // 2
    inverses = radial_inverses.reshape(M, NR, NR)
    orders = slot_order(M)
    values = grid.astype(jnp.float32).reshape(NR, NLAT, M, 2, 2)
    rotation = (omega[:, :, None] * orders.astype(jnp.float32)[None, None, :])[..., None]
    real_part = values[..., 0]
    imag_part = values[..., 1]
    forced = jnp.stack([real_part + rotation * imag_part, imag_part - rotation * real_part], -1)
    forced = forced.astype(jnp.bfloat16)
    widened = lax.optimization_barrier(forced).astype(jnp.float32).reshape(NR, NLAT, M, 4)
    northern = widened[:, :half_lats]
    southern = widened[:, half_lats:][:, ::-1]
    symmetric = lax.optimization_barrier((northern + southern).astype(jnp.bfloat16)).astype(jnp.float32)
    antisym = lax.optimization_barrier((northern - southern).astype(jnp.bfloat16)).astype(jnp.float32)
    sym_slots = jnp.transpose(symmetric, (2, 1, 0, 3)).reshape(M, half_lats, NR * 4)
    anti_slots = jnp.transpose(antisym, (2, 1, 0, 3)).reshape(M, half_lats, NR * 4)
    even_order = (orders % 2 == 0)[:, None, None]
    even_input = jnp.where(even_order, sym_slots, anti_slots)
    odd_input = jnp.where(even_order, anti_slots, sym_slots)

    def one_slot(operands):
        weights, even_data, odd_data = operands
        widened_weights = weights.astype(jnp.float32).reshape(M // 2, 2, half_lats)
        even_part = jnp.dot(widened_weights[:, 0], even_data, precision=lax.Precision.HIGHEST)
        odd_part = jnp.dot(widened_weights[:, 1], odd_data, precision=lax.Precision.HIGHEST)
        spectrum = jnp.stack([even_part, odd_part], 1).reshape(M, NR, 4)
        solved = jnp.einsum('lab,lbc->lac', inverses, spectrum, precision=lax.Precision.HIGHEST)
        return solved.reshape(M, NR * 4).astype(jnp.bfloat16)

    return lax.map(one_slot, (legendre_weights, even_input, odd_input))
```

```python
import functools

import jax
import jax.numpy as jnp
from jax import lax
from jax.experimental import pallas as pl
from jax.experimental.pallas import tpu as pltpu
from jax.sharding import PartitionSpec as P

MESH = pl.DeviceIdType.MESH
F32 = jnp.float32
BF16 = jnp.bfloat16
ROWS = 4
LANES = 128


def dot(a, b):
    return jnp.dot(a, b, preferred_element_type=F32)


def iota(shape, dim):
    return lax.broadcasted_iota(jnp.int32, shape, dim)


def one_hot(target, width):
    return jnp.where(target == iota((target.shape[0], width), 1), 1.0, 0.0).astype(BF16)


def kernel(
    tasks, grid_hbm, omega_ref, weights_hbm, inverses_hbm, out_ref,
    grid_v, omega_v, send, recv, weights, flat_inverses, paired_inverses,
    flip, spread, sym_anti, spec_send, spec_recv, merge, upper, lower, upper_out, lower_out, finish,
    grid_sem, inv_sem, own_sem, send_sem, recv_sem, wsend_sem, wrecv_sem, ysend_sem, yrecv_sem, yown_sem,
):
    row = lax.axis_index("row")
    task = lax.axis_index("ta")
    block = tasks
    half_lats = 4 * tasks
    orders = 8 * tasks
    groups = tasks // 4
    diagonal = (4 * task) // block

    def alive(unit, r):
        if unit == 0:
            return True
        return r >= diagonal if unit == 1 else r <= diagonal

    def when(condition):
        return (lambda f: f()) if condition is True else pl.when(condition)

    barrier = pltpu.get_barrier_semaphore()

    @pl.loop(1, tasks)
    def _(offset):
        pl.semaphore_signal(barrier, 1, device_id={"ta": lax.rem(task + offset, tasks)}, device_id_type=MESH)

    for offset in range(1, ROWS):
        pl.semaphore_signal(barrier, 1, device_id={"row": lax.rem(row + offset, ROWS)}, device_id_type=MESH)

    grid_copy = pltpu.make_async_copy(grid_hbm, grid_v, grid_sem)
    grid_copy.start()

    def unit_source(unit, u):
        slot = 2 * u + (1 if unit == 2 else 0)
        first = 0 if unit == 1 else block
        return weights_hbm.at[slot, pl.ds(first, block), :]

    for unit in range(3):
        for u in range(4):
            pltpu.make_async_copy(unit_source(unit, u), weights.at[unit, row, u], own_sem).start()
    for i in range(32):
        pltpu.make_async_copy(
            inverses_hbm.at[:, pl.ds(i * LANES, LANES)], flat_inverses.at[:, i, :], inv_sem
        ).start()

    for r in range(16):
        omega_v[pl.ds(8 * r, 8), :] = jnp.broadcast_to(omega_ref[:, r : r + 1], (8, LANES))
    grid_copy.wait()

    @pl.loop(0, groups)
    def _(group):
        lanes = pl.ds(pl.multiple_of(group * LANES, LANES), LANES)
        values = grid_v[:, :, lanes].astype(F32).reshape(16 * 8, LANES)
        lane = iota((1, LANES), 1)
        slot = group * 32 + lane // 4
        order = jnp.where(slot % 2 == 0, slot // 2, orders - 1 - slot // 2).astype(F32)
        partner = jnp.where(lane % 2 == 0, pltpu.roll(values, LANES - 1, 1), -pltpu.roll(values, 1, 1))
        forced = values + (omega_v[...] * order) * partner
        t0, t1, t2, t3 = (forced[32 * q : 32 * q + 32] for q in range(4))
        left = lane < 64
        a0 = jnp.where(left, t0, pltpu.roll(t2, 64, 1))
        a2 = jnp.where(left, pltpu.roll(t0, 64, 1), t2)
        a1 = jnp.where(left, t1, pltpu.roll(t3, 64, 1))
        a3 = jnp.where(left, pltpu.roll(t1, 64, 1), t3)
        first = (lane // 32) % 2 == 0
        packed = (
            jnp.where(first, a0, pltpu.roll(a1, 32, 1)),
            jnp.where(first, pltpu.roll(a0, 96, 1), a1),
            jnp.where(first, a2, pltpu.roll(a3, 32, 1)),
            jnp.where(first, pltpu.roll(a2, 96, 1), a3),
        )
        for d in range(4):
            send[group * 4 + d, :, :LANES] = packed[d][:16].astype(BF16)
            send[group * 4 + d, :, LANES:] = packed[d][16:].astype(BF16)

    pl.semaphore_wait(barrier, tasks - 1 + ROWS - 1)

    for offset in range(1, ROWS):
        for unit in range(3):

            @when(alive(unit, row))
            def _():
                for u in range(4):
                    pltpu.make_async_remote_copy(
                        src_ref=unit_source(unit, u),
                        dst_ref=weights.at[unit, row, u],
                        send_sem=wsend_sem.at[unit],
                        recv_sem=wrecv_sem.at[offset, unit],
                        device_id={"row": lax.rem(row + offset, ROWS)},
                        device_id_type=MESH,
                    ).start()

    @pl.loop(1, tasks)
    def _(step):
        to = lax.rem(task + step, tasks)
        pltpu.make_async_remote_copy(
            src_ref=send.at[to],
            dst_ref=recv.at[task],
            send_sem=send_sem,
            recv_sem=recv_sem,
            device_id={"ta": to},
            device_id_type=MESH,
        ).start()

    recv[task] = send[task]

    n = half_lats
    flip[...] = one_hot(n - 1 - iota((n, 1), 0), n)
    index = iota((256, 1), 0)
    s, c = (index // 4) % 8, index % 4
    for h in range(2):
        for high in range(2):
            radius = 4 * ((index // 32) % 4) + 2 * (index // LANES) + h
            spread[h, high] = one_hot(jnp.where(s % 2 == high, (s // 2) * 64 + c * 16 + radius, -1), 256)
    index = iota((512, 1), 0)
    for second in range(2):
        column = ((index // 16) % 4) * 64 + (index // LANES) * 16 + index % 16
        merge[second] = one_hot(jnp.where((index // 64) % 2 == second, column, -1), 256)
    index = iota((256, 1), 0)
    kind = (index // 32) % 4
    finish[...] = one_hot((2 * (index % 32) + kind % 2) * 4 + (index // LANES) * 2 + kind // 2, 256)
    upper[...] = jnp.zeros_like(upper)
    lower[...] = jnp.zeros_like(lower)
    for u in range(4):
        out_ref[2 * u + 1, :block, :] = jnp.zeros((block, 256), BF16)

    pltpu.make_async_copy(flat_inverses, flat_inverses, inv_sem).wait()

    @pl.loop(0, 2 * block)
    def _(k):
        b = flat_inverses[k]
        rolled = pltpu.roll(b, 64, 1)
        left = iota((1, LANES), 1) < 64
        paired_inverses[k] = jnp.concatenate(
            [jnp.where(left, b, 0.0), jnp.where(left, rolled, 0.0), jnp.where(left, 0.0, rolled), jnp.where(left, 0.0, b)], 0
        ).astype(BF16)

    pltpu.make_async_copy(weights.at[:, 0], weights.at[:, 0], own_sem).wait()
    for offset in range(1, ROWS):
        source = lax.rem(row + ROWS - offset, ROWS)
        for unit in range(3):

            @when(alive(unit, source))
            def _():
                pltpu.make_async_copy(
                    weights.at[unit, source], weights.at[unit, source], wrecv_sem.at[offset, unit]
                ).wait()

    pltpu.make_async_copy(recv.at[pl.ds(0, tasks - 1)], recv.at[pl.ds(0, tasks - 1)], recv_sem).wait()

    parts = []
    for h in range(2):
        arrived = recv[...].astype(F32)[:, 8 * h : 8 * h + 8, :].reshape(2 * half_lats, 256)
        northern = arrived[:half_lats]
        southern = dot(flip[...], arrived[half_lats:].astype(BF16))
        parts.append(((northern + southern).astype(BF16), (northern - southern).astype(BF16)))
    for high in range(2):
        for which in range(2):
            columns = dot(parts[0][which], spread[0, high]) + dot(parts[1][which], spread[1, high])
            columns = columns.astype(BF16)
            for pair in range(2):
                sym_anti[high, pair, :, pl.ds(which * LANES, LANES)] = columns[:, pair * LANES : (pair + 1) * LANES]

    even_row = iota((4 * block, 1), 0) % 2 == 0
    left = iota((1, LANES), 1) < 64
    for unit in range(3):
        high = 1 if unit == 2 else 0
        for pair in range(2):
            data = sym_anti[high, pair]
            results = []
            for which in range(2):
                both = dot(weights[unit, :, 2 * pair + which].reshape(4 * block, half_lats), data)
                even_order = (which + high) % 2 == 0
                first, second = both[:, :LANES], both[:, LANES:]
                results.append(jnp.where(even_row, first, second) if even_order else jnp.where(even_row, second, first))
            merged = jnp.where(left, results[0], results[1]).astype(BF16)
            spec_send[unit, :, pair] = merged.reshape(4, block, LANES)
        for offset in range(1, ROWS):
            to = lax.rem(row + offset, ROWS)

            @when(alive(unit, to))
            def _():
                pltpu.make_async_remote_copy(
                    src_ref=spec_send.at[unit, to],
                    dst_ref=spec_recv.at[unit, row],
                    send_sem=ysend_sem.at[unit, offset],
                    recv_sem=yrecv_sem.at[unit, offset],
                    device_id={"row": to},
                    device_id_type=MESH,
                ).start()

    spec_recv[:, row] = spec_send[:, row]

    for unit in range(3):

        @when(alive(unit, row))
        def _():
            for offset in range(1, ROWS):
                source = lax.rem(row + ROWS - offset, ROWS)
                pltpu.make_async_copy(
                    spec_recv.at[unit, source], spec_recv.at[unit, source], yrecv_sem.at[unit, offset]
                ).wait()
            for pair in range(2):
                joined = jnp.concatenate([spec_recv[unit, r, pair] for r in range(ROWS)], 1)
                for second in range(2):
                    spectrum = dot(joined, merge[second])
                    for field in range(2):
                        place = (2 * pair + second) * 2 + field
                        part = spectrum[:, field * LANES : (field + 1) * LANES]
                        if unit == 1:
                            lower[pl.ds(place, block, stride=8), :] = part
                        else:
                            upper[pl.ds(place + (8 if unit == 2 else 0), block, stride=16), :] = part

    def solve(lhs, k):
        return lax.dot_general(
            lhs.astype(BF16), paired_inverses[k], (((1,), (1,)), ((), ())), preferred_element_type=F32
        )

    @pl.loop(0, block)
    def _(k):
        solved = solve(upper[pl.ds(pl.multiple_of(k * 16, 16), 16), :], block + k)
        upper_out[pl.ds(k, 16, stride=block), :] = solved

    @pl.loop(0, block)
    def _(k):
        solved = solve(lower[pl.ds(pl.multiple_of(k * 8, 8), 8), :], k)
        lower_out[pl.ds(k, 8, stride=block), :] = solved

    def ordered(ref, place):
        fields = [ref[pl.ds((place + field) * block, block), :] for field in range(2)]
        return dot(jnp.concatenate(fields, 1).astype(BF16), finish[...]).astype(BF16)

    for u in range(4):
        out_ref[2 * u, block:, :] = ordered(upper_out, 2 * u)
        out_ref[2 * u + 1, block:, :] = ordered(upper_out, 8 + 2 * u)
        out_ref[2 * u, :block, :] = ordered(lower_out, 2 * u)

    pltpu.make_async_copy(send.at[pl.ds(0, tasks - 1)], send.at[pl.ds(0, tasks - 1)], send_sem).wait()
    for unit in range(3):

        @when(alive(unit, row))
        def _():
            three = weights.at[unit, pl.ds(0, 3)]
            pltpu.make_async_copy(three, three, wsend_sem.at[unit]).wait()

        for offset in range(1, ROWS):
            to = lax.rem(row + offset, ROWS)

            @when(alive(unit, to))
            def _():
                sent = spec_send.at[unit, to]
                pltpu.make_async_copy(sent, sent, ysend_sem.at[unit, offset]).wait()


def shards(tasks, grid, omega, legendre_weights, radial_inverses):
    block = tasks
    half_lats = 4 * tasks
    any_space = pl.BlockSpec(memory_space=pl.ANY)
    in_vmem = pl.BlockSpec(memory_space=pltpu.VMEM)
    dma = pltpu.SemaphoreType.DMA
    return pl.pallas_call(
        functools.partial(kernel, tasks),
        out_shape=jax.ShapeDtypeStruct(legendre_weights.shape[:2] + (256,), BF16),
        in_specs=[any_space, in_vmem, any_space, any_space],
        out_specs=in_vmem,
        scratch_shapes=[
            pltpu.VMEM((16, 8, 32 * tasks), BF16),
            pltpu.VMEM((128, LANES), F32),
            pltpu.VMEM((tasks, 16, 256), BF16),
            pltpu.VMEM((tasks, 16, 256), BF16),
            pltpu.VMEM((3, ROWS, 4, block, half_lats), BF16),
            pltpu.VMEM((2 * block, 32, LANES), F32),
            pltpu.VMEM((2 * block, LANES, LANES), BF16),
            pltpu.VMEM((half_lats, half_lats), BF16),
            pltpu.VMEM((2, 2, 256, 256), BF16),
            pltpu.VMEM((2, 2, half_lats, 256), BF16),
            pltpu.VMEM((3, ROWS, 2, block, LANES), BF16),
            pltpu.VMEM((3, ROWS, 2, block, LANES), BF16),
            pltpu.VMEM((2, 512, 256), BF16),
            pltpu.VMEM((block * 16, LANES), F32),
            pltpu.VMEM((block * 8, LANES), F32),
            pltpu.VMEM((block * 16, LANES), F32),
            pltpu.VMEM((block * 8, LANES), F32),
            pltpu.VMEM((256, 256), BF16),
            dma, dma, dma, dma, dma,
            dma((3,)), dma((ROWS, 3)), dma((3, ROWS)), dma((3, ROWS)), dma,
        ],
        compiler_params=pltpu.CompilerParams(
            collective_id=0, has_side_effects=True, vmem_limit_bytes=48 * 1024 * 1024
        ),
    )(grid, omega.T, legendre_weights, radial_inverses)


def solution(mesh):
    in_specs = (P("row", "ta", None), P("row", "ta"), P("ta", "row", None), P("row", None))
    out_specs = P("ta", "row", None)
    return jax.shard_map(
        functools.partial(shards, mesh.shape["ta"]), mesh=mesh, in_specs=in_specs, out_specs=out_specs, check_vma=False
    )
```

```python
import functools

import jax
import jax.numpy as jnp
from jax import lax
from jax.experimental import pallas as pl
from jax.experimental.pallas import tpu as pltpu
from jax.sharding import PartitionSpec as P

MESH = pl.DeviceIdType.MESH
F32 = jnp.float32
BF16 = jnp.bfloat16
ROWS = 4
LANES = 128


def dot(a, b):
    return jnp.dot(a, b, preferred_element_type=F32)


def iota(shape, dim):
    return lax.broadcasted_iota(jnp.int32, shape, dim)


def one_hot(target, width):
    return jnp.where(target == iota((target.shape[0], width), 1), 1.0, 0.0).astype(BF16)


def kernel(
    tasks, grid_hbm, omega_hbm, weights_hbm, inverses_hbm, out_ref,
    grid_v, omega_ref, omega_v, send, recv, weights, flat_inverses, paired_inverses,
    flip, spread, sym_anti, spec_send, spec_recv, merge, upper, lower, upper_out, lower_out, finish,
    grid_sem, omega_sem, inv_sem, own_sem, send_sem, recv_sem, wsend_sem, wrecv_sem, wrelay_sem, ysend_sem, yrecv_sem, ready_sem,
):
    row = lax.axis_index("row")
    task = lax.axis_index("ta")
    block = tasks
    half_lats = 4 * tasks
    orders = 8 * tasks
    groups = tasks // 4
    diagonal = (4 * task) // block

    def alive(unit, r):
        if unit == 0:
            return True
        return r >= diagonal if unit == 1 else r <= diagonal

    def when(condition):
        return (lambda f: f()) if condition is True else pl.when(condition)

    barrier = pltpu.get_barrier_semaphore()


    planes = max(tasks // 8, 1)
    width = tasks // planes
    levels = planes // 2 + 1
    plane, place = task // width, task % width

    def distance(z):
        return z + z // levels * (planes - 2 * z)

    level = distance(plane)

    def peers(lev, act):
        for side in range(2):
            z = lev if side == 0 else planes - lev

            @pl.when((side == 0) | ((lev > 0) & (2 * lev < planes)))
            def _():
                @pl.loop(0, width)
                def _(i):
                    to = z * width + lax.rem(place + i, width)

                    @pl.when(to != task)
                    def _():
                        act(to)

    @pl.loop(level, levels)
    def _(lev):
        peers(lev, lambda to: pl.semaphore_signal(barrier, 1, device_id={"ta": to}, device_id_type=MESH))

    for offset in range(1, ROWS):
        pl.semaphore_signal(barrier, 1, device_id={"row": lax.rem(row + offset, ROWS)}, device_id_type=MESH)

    grid_copy = pltpu.make_async_copy(grid_hbm, grid_v, grid_sem)
    grid_copy.start()
    omega_copy = pltpu.make_async_copy(omega_hbm, omega_ref, omega_sem)
    omega_copy.start()

    def unit_source(unit, u):
        slot = 2 * u + (1 if unit == 2 else 0)
        first = 0 if unit == 1 else block
        return weights_hbm.at[slot, pl.ds(first, block), :]

    for unit in range(3):
        for u in range(4):
            pltpu.make_async_copy(unit_source(unit, u), weights.at[unit, row, u], own_sem).start()
    for i in range(32):
        pltpu.make_async_copy(
            inverses_hbm.at[:, pl.ds(i * LANES, LANES)], flat_inverses.at[:, i, :], inv_sem
        ).start()

    known = 2 * level + 1
    pl.semaphore_wait(barrier, (known - known // (planes + 1)) * width - 1 + ROWS - 1)

    @pl.loop(0, level)
    def _(lev):
        peers(lev, lambda to: pl.semaphore_signal(ready_sem.at[level], 1, device_id={"ta": to}, device_id_type=MESH))


    for offset in (1, ROWS - 1):
        for unit in range(3):

            @when(alive(unit, row))
            def _():
                for u in range(4):
                    pltpu.make_async_remote_copy(
                        src_ref=unit_source(unit, u),
                        dst_ref=weights.at[unit, row, u],
                        send_sem=wsend_sem.at[unit],
                        recv_sem=wrecv_sem.at[offset, unit],
                        device_id={"row": lax.rem(row + offset, ROWS)},
                        device_id_type=MESH,
                    ).start()

    omega_copy.wait()
    for r in range(16):
        omega_v[pl.ds(8 * r, 8), :] = jnp.broadcast_to(omega_ref[:, r : r + 1], (8, LANES))
    grid_copy.wait()

    @pl.loop(0, groups)
    def _(group):
        lanes = pl.ds(pl.multiple_of(group * LANES, LANES), LANES)
        values = grid_v[:, :, lanes].astype(F32).reshape(16 * 8, LANES)
        lane = iota((1, LANES), 1)
        slot = group * 32 + lane // 4
        order = jnp.where(slot % 2 == 0, slot // 2, orders - 1 - slot // 2).astype(F32)
        partner = jnp.where(lane % 2 == 0, pltpu.roll(values, LANES - 1, 1), -pltpu.roll(values, 1, 1))
        forced = values + (omega_v[...] * order) * partner
        t0, t1, t2, t3 = (forced[32 * q : 32 * q + 32] for q in range(4))
        left = lane < 64
        a0 = jnp.where(left, t0, pltpu.roll(t2, 64, 1))
        a2 = jnp.where(left, pltpu.roll(t0, 64, 1), t2)
        a1 = jnp.where(left, t1, pltpu.roll(t3, 64, 1))
        a3 = jnp.where(left, pltpu.roll(t1, 64, 1), t3)
        first = (lane // 32) % 2 == 0
        packed = (
            jnp.where(first, a0, pltpu.roll(a1, 32, 1)),
            jnp.where(first, pltpu.roll(a0, 96, 1), a1),
            jnp.where(first, a2, pltpu.roll(a3, 32, 1)),
            jnp.where(first, pltpu.roll(a2, 96, 1), a3),
        )
        for d in range(4):
            send[group * 4 + d, :, :LANES] = packed[d][:16].astype(BF16)
            send[group * 4 + d, :, LANES:] = packed[d][16:].astype(BF16)

    def deliver(to):
        pltpu.make_async_remote_copy(
            src_ref=send.at[to],
            dst_ref=recv.at[task],
            send_sem=send_sem,
            recv_sem=recv_sem,
            device_id={"ta": to},
            device_id_type=MESH,
        ).start()

    for lev in range(levels):

        @pl.when(lev > level)
        def _():
            pl.semaphore_wait(ready_sem.at[lev], width * (2 if 0 < 2 * lev < planes else 1))

        peers(lev, deliver)

    recv[task] = send[task]

    n = half_lats
    flip[...] = one_hot(n - 1 - iota((n, 1), 0), n)
    index = iota((256, 1), 0)
    s, c = (index // 4) % 8, index % 4
    for h in range(2):
        for high in range(2):
            radius = 4 * ((index // 32) % 4) + 2 * (index // LANES) + h
            spread[h, high] = one_hot(jnp.where(s % 2 == high, (s // 2) * 64 + c * 16 + radius, -1), 256)
    index = iota((512, 1), 0)
    for second in range(2):
        column = ((index // 16) % 4) * 64 + (index // LANES) * 16 + index % 16
        merge[second] = one_hot(jnp.where((index // 64) % 2 == second, column, -1), 256)
    index = iota((256, 1), 0)
    kind = (index // 32) % 4
    finish[...] = one_hot((2 * (index % 32) + kind % 2) * 4 + (index // LANES) * 2 + kind // 2, 256)
    upper[...] = jnp.zeros_like(upper)
    lower[...] = jnp.zeros_like(lower)
    for u in range(4):
        out_ref[2 * u + 1, :block, :] = jnp.zeros((block, 256), BF16)

    pltpu.make_async_copy(flat_inverses, flat_inverses, inv_sem).wait()

    def pair_inverses(start):
        @pl.loop(start // 4, (start + block) // 4)
        def _(step):
            for i in range(4):
                k = step * 4 + i
                b = flat_inverses[k]
                rolled = pltpu.roll(b, 64, 1)
                left = iota((1, LANES), 1) < 64
                quarters = (
                    jnp.where(left, b, 0.0), jnp.where(left, rolled, 0.0),
                    jnp.where(left, 0.0, rolled), jnp.where(left, 0.0, b),
                )
                paired_inverses[k] = jnp.concatenate(quarters, 0).astype(BF16)

    def relay(unit, source, to):
        @when(alive(unit, source))
        def _():
            block_ref = weights.at[unit, source]
            pltpu.make_async_copy(block_ref, block_ref, wrecv_sem.at[1 if unit == 0 else 3, unit]).wait()
            pltpu.make_async_remote_copy(
                src_ref=block_ref,
                dst_ref=block_ref,
                send_sem=wrelay_sem.at[unit],
                recv_sem=wrecv_sem.at[2, unit],
                device_id={"row": to},
                device_id_type=MESH,
            ).start()

    right, left_row, across = (lax.rem(row + i, ROWS) for i in (1, 3, 2))
    pair_inverses(0)
    relay(0, left_row, right)
    relay(1, right, left_row)
    relay(2, right, left_row)
    pair_inverses(block)

    pltpu.make_async_copy(weights.at[:, 0], weights.at[:, 0], own_sem).wait()
    for offset, source in ((1, left_row), (2, across), (3, right)):
        for unit in range(3):
            if offset != 2 and (offset == 1) == (unit == 0):
                continue

            @when(alive(unit, source))
            def _():
                block_ref = weights.at[unit, source]
                pltpu.make_async_copy(block_ref, block_ref, wrecv_sem.at[offset, unit]).wait()

    pltpu.make_async_copy(recv.at[pl.ds(0, tasks - 1)], recv.at[pl.ds(0, tasks - 1)], recv_sem).wait()

    parts = []
    for h in range(2):
        arrived = recv[...].astype(F32)[:, 8 * h : 8 * h + 8, :].reshape(2 * half_lats, 256)
        northern = arrived[:half_lats]
        southern = dot(flip[...], arrived[half_lats:].astype(BF16))
        parts.append(((northern + southern).astype(BF16), (northern - southern).astype(BF16)))
    for high in range(2):
        for which in range(2):
            columns = dot(parts[0][which], spread[0, high]) + dot(parts[1][which], spread[1, high])
            columns = columns.astype(BF16)
            for pair in range(2):
                sym_anti[high, pair, :, pl.ds(which * LANES, LANES)] = columns[:, pair * LANES : (pair + 1) * LANES]

    even_row = iota((4 * block, 1), 0) % 2 == 0
    left = iota((1, LANES), 1) < 64
    for unit in range(3):
        high = 1 if unit == 2 else 0
        for pair in range(2):
            data = sym_anti[high, pair]
            results = []
            for which in range(2):
                both = dot(weights[unit, :, 2 * pair + which].reshape(4 * block, half_lats), data)
                even_order = (which + high) % 2 == 0
                first, second = both[:, :LANES], both[:, LANES:]
                results.append(jnp.where(even_row, first, second) if even_order else jnp.where(even_row, second, first))
            merged = jnp.where(left, results[0], results[1]).astype(BF16)
            spec_send[unit, :, pair] = merged.reshape(4, block, LANES)
        for offset in range(1, ROWS):
            to = lax.rem(row + offset, ROWS)

            @when(alive(unit, to))
            def _():
                pltpu.make_async_remote_copy(
                    src_ref=spec_send.at[unit, to],
                    dst_ref=spec_recv.at[unit, row],
                    send_sem=ysend_sem.at[unit, offset],
                    recv_sem=yrecv_sem.at[unit, offset],
                    device_id={"row": to},
                    device_id_type=MESH,
                ).start()

    spec_recv[:, row] = spec_send[:, row]

    for unit in range(3):

        @when(alive(unit, row))
        def _():
            for offset in range(1, ROWS):
                source = lax.rem(row + ROWS - offset, ROWS)
                pltpu.make_async_copy(
                    spec_recv.at[unit, source], spec_recv.at[unit, source], yrecv_sem.at[unit, offset]
                ).wait()
            for pair in range(2):
                joined = jnp.concatenate([spec_recv[unit, r, pair] for r in range(ROWS)], 1)
                for second in range(2):
                    spectrum = dot(joined, merge[second])
                    for field in range(2):
                        place = (2 * pair + second) * 2 + field
                        part = spectrum[:, field * LANES : (field + 1) * LANES]
                        if unit == 1:
                            lower[pl.ds(place, block, stride=8), :] = part
                        else:
                            upper[pl.ds(place + (8 if unit == 2 else 0), block, stride=16), :] = part

    def solve(lhs, k):
        return lax.dot_general(
            lhs.astype(BF16), paired_inverses[k], (((1,), (1,)), ((), ())), preferred_element_type=F32
        )

    @pl.loop(0, block // 4)
    def _(step):
        for i in range(4):
            k = step * 4 + i
            solved = solve(upper[pl.ds(pl.multiple_of(k * 16, 16), 16), :], block + k)
            upper_out[pl.ds(k, 16, stride=block), :] = solved
            solved = solve(lower[pl.ds(pl.multiple_of(k * 8, 8), 8), :], k)
            lower_out[pl.ds(k, 8, stride=block), :] = solved

    def ordered(ref, place):
        fields = [ref[pl.ds((place + field) * block, block), :] for field in range(2)]
        return dot(jnp.concatenate(fields, 1).astype(BF16), finish[...]).astype(BF16)

    for u in range(4):
        out_ref[2 * u, block:, :] = ordered(upper_out, 2 * u)
        out_ref[2 * u + 1, block:, :] = ordered(upper_out, 8 + 2 * u)
        out_ref[2 * u, :block, :] = ordered(lower_out, 2 * u)

    pltpu.make_async_copy(send.at[pl.ds(0, tasks - 1)], send.at[pl.ds(0, tasks - 1)], send_sem).wait()
    for unit in range(3):

        @when(alive(unit, row))
        def _():
            sent = weights.at[unit, pl.ds(0, 2)]
            pltpu.make_async_copy(sent, sent, wsend_sem.at[unit]).wait()

        @when(alive(unit, left_row if unit == 0 else right))
        def _():
            sent = weights.at[unit, 0]
            pltpu.make_async_copy(sent, sent, wrelay_sem.at[unit]).wait()

        for offset in range(1, ROWS):
            to = lax.rem(row + offset, ROWS)

            @when(alive(unit, to))
            def _():
                sent = spec_send.at[unit, to]
                pltpu.make_async_copy(sent, sent, ysend_sem.at[unit, offset]).wait()


def shards(tasks, grid, omega, legendre_weights, radial_inverses):
    block = tasks
    half_lats = 4 * tasks
    in_hbm = pl.BlockSpec(memory_space=pltpu.HBM)
    in_vmem = pl.BlockSpec(memory_space=pltpu.VMEM)
    dma = pltpu.SemaphoreType.DMA
    return pl.pallas_call(
        functools.partial(kernel, tasks),
        out_shape=jax.ShapeDtypeStruct(legendre_weights.shape[:2] + (256,), BF16),
        in_specs=[in_hbm] * 4,
        out_specs=in_vmem,
        scratch_shapes=[
            pltpu.VMEM((16, 8, 32 * tasks), BF16),
            pltpu.VMEM((8, 16), F32),
            pltpu.VMEM((128, LANES), F32),
            pltpu.VMEM((tasks, 16, 256), BF16),
            pltpu.VMEM((tasks, 16, 256), BF16),
            pltpu.VMEM((3, ROWS, 4, block, half_lats), BF16),
            pltpu.VMEM((2 * block, 32, LANES), F32),
            pltpu.VMEM((2 * block, LANES, LANES), BF16),
            pltpu.VMEM((half_lats, half_lats), BF16),
            pltpu.VMEM((2, 2, 256, 256), BF16),
            pltpu.VMEM((2, 2, half_lats, 256), BF16),
            pltpu.VMEM((3, ROWS, 2, block, LANES), BF16),
            pltpu.VMEM((3, ROWS, 2, block, LANES), BF16),
            pltpu.VMEM((2, 512, 256), BF16),
            pltpu.VMEM((block * 16, LANES), F32),
            pltpu.VMEM((block * 8, LANES), F32),
            pltpu.VMEM((block * 16, LANES), F32),
            pltpu.VMEM((block * 8, LANES), F32),
            pltpu.VMEM((256, 256), BF16),
            dma, dma, dma, dma, dma, dma,
            dma((3,)), dma((ROWS, 3)), dma((3,)), dma((3, ROWS)), dma((3, ROWS)),
            pltpu.SemaphoreType.REGULAR((5,)),
        ],
        compiler_params=pltpu.CompilerParams(
            collective_id=0, has_side_effects=True, vmem_limit_bytes=60 * 1024 * 1024
        ),
    )(grid, omega.T, legendre_weights, radial_inverses)


def solution(mesh):
    in_specs = (P("row", "ta", None), P("row", "ta"), P("ta", "row", None), P("row", None))
    out_specs = P("ta", "row", None)
    return jax.shard_map(
        functools.partial(shards, mesh.shape["ta"]), mesh=mesh, in_specs=in_specs, out_specs=out_specs, check_vma=False
    )
```

```python
import functools

import jax
import jax.numpy as jnp
from jax import lax
from jax.experimental import pallas as pl
from jax.experimental.pallas import tpu as pltpu
from jax.sharding import PartitionSpec as P

MESH = pl.DeviceIdType.MESH
F32 = jnp.float32
BF16 = jnp.bfloat16
ROWS = 4
LANES = 128


def dot(a, b):
    return jnp.dot(a, b, preferred_element_type=F32)


def iota(shape, dim):
    return lax.broadcasted_iota(jnp.int32, shape, dim)


def one_hot(target, width):
    return jnp.where(target == iota((target.shape[0], width), 1), 1.0, 0.0).astype(BF16)


def kernel(
    tasks, grid_hbm, omega_hbm, weights_hbm, inverses_hbm, out_ref,
    grid_v, omega_ref, omega_v, send, recv, weights, flat_inverses, paired_inverses,
    flip, spread, sym_anti, spec_send, spec_recv, merge, spectra, solved, finish,
    grid_sem, omega_sem, inv_sem, own_sem, send_sem, recv_sem, wsend_sem, wrecv_sem, wrelay_sem, ysend_sem, yrecv_sem,
):
    row = lax.axis_index("row")
    task = lax.axis_index("ta")
    block = tasks
    half_lats = 4 * tasks
    orders = 8 * tasks
    groups = tasks // 4
    diagonal = (4 * task) // block

    def alive(unit, r):
        if unit == 0:
            return True
        return r >= diagonal if unit == 1 else r <= diagonal

    def when(condition):
        return (lambda f: f()) if condition is True else pl.when(condition)

    barrier = pltpu.get_barrier_semaphore()

    @pl.loop(1, tasks)
    def _(offset):
        pl.semaphore_signal(barrier, 1, device_id={"ta": lax.rem(task + offset, tasks)}, device_id_type=MESH)

    for offset in range(1, ROWS):
        pl.semaphore_signal(barrier, 1, device_id={"row": lax.rem(row + offset, ROWS)}, device_id_type=MESH)

    grid_copy = pltpu.make_async_copy(grid_hbm, grid_v, grid_sem)
    grid_copy.start()
    omega_copy = pltpu.make_async_copy(omega_hbm, omega_ref, omega_sem)
    omega_copy.start()

    def unit_source(unit, u):
        slot = 2 * u + (1 if unit == 2 else 0)
        first = 0 if unit == 1 else block
        return weights_hbm.at[slot, pl.ds(first, block), :]

    for unit in range(3):
        for u in range(4):
            pltpu.make_async_copy(unit_source(unit, u), weights.at[unit, row, u], own_sem).start()
    for i in range(32):
        pltpu.make_async_copy(
            inverses_hbm.at[:, pl.ds(i * LANES, LANES)], flat_inverses.at[:, i, :], inv_sem
        ).start()

    omega_copy.wait()
    for r in range(16):
        omega_v[pl.ds(8 * r, 8), :] = jnp.broadcast_to(omega_ref[:, r : r + 1], (8, LANES))
    grid_copy.wait()

    @pl.loop(0, groups)
    def _(group):
        lanes = pl.ds(pl.multiple_of(group * LANES, LANES), LANES)
        values = grid_v[:, :, lanes].astype(F32).reshape(16 * 8, LANES)
        lane = iota((1, LANES), 1)
        slot = group * 32 + lane // 4
        order = jnp.where(slot % 2 == 0, slot // 2, orders - 1 - slot // 2).astype(F32)
        partner = jnp.where(lane % 2 == 0, pltpu.roll(values, LANES - 1, 1), -pltpu.roll(values, 1, 1))
        forced = values + (omega_v[...] * order) * partner
        t0, t1, t2, t3 = (forced[32 * q : 32 * q + 32] for q in range(4))
        left = lane < 64
        a0 = jnp.where(left, t0, pltpu.roll(t2, 64, 1))
        a2 = jnp.where(left, pltpu.roll(t0, 64, 1), t2)
        a1 = jnp.where(left, t1, pltpu.roll(t3, 64, 1))
        a3 = jnp.where(left, pltpu.roll(t1, 64, 1), t3)
        first = (lane // 32) % 2 == 0
        packed = (
            jnp.where(first, a0, pltpu.roll(a1, 32, 1)),
            jnp.where(first, pltpu.roll(a0, 96, 1), a1),
            jnp.where(first, a2, pltpu.roll(a3, 32, 1)),
            jnp.where(first, pltpu.roll(a2, 96, 1), a3),
        )
        low = (lane // 4) % 2 == 0
        for d in range(4):
            near, far = packed[d][:16], packed[d][16:]
            send[0, group * 4 + d] = jnp.where(low, near, pltpu.roll(far, 4, 1)).astype(BF16)
            send[1, group * 4 + d] = jnp.where(low, pltpu.roll(near, LANES - 4, 1), far).astype(BF16)

    pl.semaphore_wait(barrier, tasks - 1 + ROWS - 1)

    pltpu.make_async_copy(weights.at[:, 0], weights.at[:, 0], own_sem).wait()
    for unit in range(3):

        @when(alive(unit, row))
        def _():
            for offset in (1, ROWS - 1):
                pltpu.make_async_remote_copy(
                    src_ref=weights.at[unit, row],
                    dst_ref=weights.at[unit, row],
                    send_sem=wsend_sem.at[unit],
                    recv_sem=wrecv_sem.at[offset, unit],
                    device_id={"row": lax.rem(row + offset, ROWS)},
                    device_id_type=MESH,
                ).start()

    def deliver(high, to):
        pltpu.make_async_remote_copy(
            src_ref=send.at[high, to],
            dst_ref=recv.at[high, task],
            send_sem=send_sem.at[high],
            recv_sem=recv_sem.at[high],
            device_id={"ta": to},
            device_id_type=MESH,
        ).start()

    planes = max(tasks // 8, 1)
    width = tasks // planes
    plane, place = task // width, task % width
    steps = sorted(range(planes), key=lambda d: -min(d, planes - d))

    for high in range(2):

        @pl.loop(0, width)
        def _(i):
            for d in steps:
                to = lax.rem(plane + d, planes) * width + lax.rem(place + i, width)

                @pl.when(to != task)
                def _():
                    deliver(high, to)

    recv[:, task] = send[:, task]

    n = half_lats
    flip[...] = one_hot(n - 1 - iota((n, 1), 0), n)
    index = iota((256, 1), 0)
    radius = 4 * ((index // 32) % 4) + 2 * ((index // 4) % 2) + index // LANES
    spread[...] = one_hot(((index // 8) % 4) * 64 + (index % 4) * 16 + radius, 256)
    index = iota((512, 1), 0)
    for second in range(2):
        column = ((index // 16) % 4) * 64 + (index // LANES) * 16 + index % 16
        merge[second] = one_hot(jnp.where((index // 64) % 2 == second, column, -1), 256)
    index = iota((256, 1), 0)
    kind = (index // 32) % 4
    finish[...] = one_hot((2 * (index % 32) + kind % 2) * 4 + (index // LANES) * 2 + kind // 2, 256)
    spectra[...] = jnp.zeros_like(spectra)
    for u in range(4):
        out_ref[2 * u + 1, :block, :] = jnp.zeros((block, 256), BF16)

    pltpu.make_async_copy(flat_inverses, flat_inverses, inv_sem).wait()

    def pair_inverses(start):
        @pl.loop(start // 4, (start + block) // 4)
        def _(step):
            lane = iota((1, LANES), 1)
            turned = flat_inverses[pl.ds(step * 4, 4)].reshape(LANES, LANES).T
            for i in range(4):
                even = pltpu.roll(turned[:64], (LANES - 32 * i) % LANES, 1)
                odd = pltpu.roll(turned[64:], (LANES + 32 - 32 * i) % LANES, 1)
                top = jnp.where(lane < 32, even, jnp.where(lane < 64, odd, 0.0))
                paired_inverses[step * 4 + i] = jnp.concatenate([top, pltpu.roll(top, 64, 1)], 0).astype(BF16)

    def relay(unit, source, to):
        @when(alive(unit, source))
        def _():
            block_ref = weights.at[unit, source]
            pltpu.make_async_copy(block_ref, block_ref, wrecv_sem.at[1 if unit == 0 else 3, unit]).wait()
            pltpu.make_async_remote_copy(
                src_ref=block_ref,
                dst_ref=block_ref,
                send_sem=wrelay_sem.at[unit],
                recv_sem=wrecv_sem.at[2, unit],
                device_id={"row": to},
                device_id_type=MESH,
            ).start()

    right, left_row, across = (lax.rem(row + i, ROWS) for i in (1, 3, 2))
    pair_inverses(0)
    relay(0, left_row, right)
    relay(1, right, left_row)
    relay(2, right, left_row)
    pair_inverses(block)

    def weights_here(unit):
        for offset, source in ((1, left_row), (2, across), (3, right)):
            if offset != 2 and (offset == 1) == (unit == 0):
                continue

            @when(alive(unit, source))
            def _():
                block_ref = weights.at[unit, source]
                pltpu.make_async_copy(block_ref, block_ref, wrecv_sem.at[offset, unit]).wait()

    def separate(high):
        rest = recv.at[high, pl.ds(0, tasks - 1)]
        pltpu.make_async_copy(rest, rest, recv_sem.at[high]).wait()
        arrived = recv[high].astype(F32)
        halves = [arrived[:, 8 * h : 8 * h + 8, :].reshape(2 * half_lats, LANES) for h in range(2)]
        northern = jnp.concatenate([half[:half_lats] for half in halves], 1)
        southern = jnp.concatenate([half[half_lats:] for half in halves], 1)
        southern = dot(flip[...], southern.astype(BF16))
        for which, part in enumerate((northern + southern, northern - southern)):
            columns = dot(part.astype(BF16), spread[...]).astype(BF16)
            for pair in range(2):
                sym_anti[high, pair, :, pl.ds(which * LANES, LANES)] = columns[:, pair * LANES : (pair + 1) * LANES]

    even_row = iota((4 * block, 1), 0) % 2 == 0
    left = iota((1, LANES), 1) < 64

    def transform(unit):
        high = 1 if unit == 2 else 0
        for pair in range(2):
            data = sym_anti[high, pair]
            results = []
            for which in range(2):
                both = dot(weights[unit, :, 2 * pair + which].reshape(4 * block, half_lats), data)
                even_order = (which + high) % 2 == 0
                first, second = both[:, :LANES], both[:, LANES:]
                results.append(jnp.where(even_row, first, second) if even_order else jnp.where(even_row, second, first))
            merged = jnp.where(left, results[0], results[1]).astype(BF16)
            spec_send[unit, :, pair] = merged.reshape(4, block, LANES)
        for offset in (2, 1, 3):
            to = lax.rem(row + offset, ROWS)

            @when(alive(unit, to))
            def _():
                pltpu.make_async_remote_copy(
                    src_ref=spec_send.at[unit, to],
                    dst_ref=spec_recv.at[unit, row],
                    send_sem=ysend_sem.at[unit, offset],
                    recv_sem=yrecv_sem.at[unit, offset],
                    device_id={"row": to},
                    device_id_type=MESH,
                ).start()

        spec_recv[unit, row] = spec_send[unit, row]

    weights_here(0)
    weights_here(1)
    separate(0)
    transform(0)
    transform(1)
    weights_here(2)
    separate(1)
    transform(2)

    def arrive(unit):
        @when(alive(unit, row))
        def _():
            for offset in range(1, ROWS):
                source = lax.rem(row + ROWS - offset, ROWS)
                pltpu.make_async_copy(
                    spec_recv.at[unit, source], spec_recv.at[unit, source], yrecv_sem.at[unit, offset]
                ).wait()
            for pair in range(2):
                joined = jnp.concatenate([spec_recv[unit, r, pair] for r in range(ROWS)], 1)
                for second in range(2):
                    spectrum = dot(joined, merge[second])
                    for field in range(2):
                        spot = (2 * pair + second) * 2 + field
                        spectra[unit, pl.ds(spot, block, stride=8), :] = spectrum[:, field * LANES : (field + 1) * LANES]

    def solve(unit):
        arrive(unit)
        start = 0 if unit == 1 else block
        unroll = min(32, block)

        @pl.loop(0, block // unroll)
        def _(step):
            for i in range(unroll):
                k = step * unroll + i
                lhs = spectra[unit, pl.ds(pl.multiple_of(k * 8, 8), 8), :].astype(BF16)
                solved[unit, pl.ds(k, 8, stride=block), :] = dot(lhs, paired_inverses[start + k])

        for u in range(4):
            fields = [solved[unit, pl.ds((2 * u + field) * block, block), :] for field in range(2)]
            result = dot(jnp.concatenate(fields, 1).astype(BF16), finish[...]).astype(BF16)
            out_ref[2 * u + (1 if unit == 2 else 0), pl.ds(start, block), :] = result

    solve(0)
    solve(1)
    solve(2)

    for high in range(2):
        sent = send.at[high, pl.ds(0, tasks - 1)]
        pltpu.make_async_copy(sent, sent, send_sem.at[high]).wait()
    for unit in range(3):

        @when(alive(unit, row))
        def _():
            sent = weights.at[unit, pl.ds(0, 2)]
            pltpu.make_async_copy(sent, sent, wsend_sem.at[unit]).wait()

        @when(alive(unit, left_row if unit == 0 else right))
        def _():
            sent = weights.at[unit, 0]
            pltpu.make_async_copy(sent, sent, wrelay_sem.at[unit]).wait()

        for offset in range(1, ROWS):
            to = lax.rem(row + offset, ROWS)

            @when(alive(unit, to))
            def _():
                sent = spec_send.at[unit, to]
                pltpu.make_async_copy(sent, sent, ysend_sem.at[unit, offset]).wait()


def shards(tasks, grid, omega, legendre_weights, radial_inverses):
    block = tasks
    half_lats = 4 * tasks
    in_hbm = pl.BlockSpec(memory_space=pltpu.HBM)
    in_vmem = pl.BlockSpec(memory_space=pltpu.VMEM)
    dma = pltpu.SemaphoreType.DMA
    return pl.pallas_call(
        functools.partial(kernel, tasks),
        out_shape=jax.ShapeDtypeStruct(legendre_weights.shape[:2] + (256,), BF16),
        in_specs=[in_hbm] * 4,
        out_specs=in_vmem,
        scratch_shapes=[
            pltpu.VMEM((16, 8, 32 * tasks), BF16),
            pltpu.VMEM((8, 16), F32),
            pltpu.VMEM((128, LANES), F32),
            pltpu.VMEM((2, tasks, 16, LANES), BF16),
            pltpu.VMEM((2, tasks, 16, LANES), BF16),
            pltpu.VMEM((3, ROWS, 4, block, half_lats), BF16),
            pltpu.VMEM((2 * block, 32, LANES), F32),
            pltpu.VMEM((2 * block, LANES, LANES), BF16),
            pltpu.VMEM((half_lats, half_lats), BF16),
            pltpu.VMEM((256, 256), BF16),
            pltpu.VMEM((2, 2, half_lats, 256), BF16),
            pltpu.VMEM((3, ROWS, 2, block, LANES), BF16),
            pltpu.VMEM((3, ROWS, 2, block, LANES), BF16),
            pltpu.VMEM((2, 512, 256), BF16),
            pltpu.VMEM((3, block * 8, LANES), F32),
            pltpu.VMEM((3, block * 8, LANES), F32),
            pltpu.VMEM((256, 256), BF16),
            dma, dma, dma, dma, dma((2,)), dma((2,)),
            dma((3,)), dma((ROWS, 3)), dma((3,)), dma((3, ROWS)), dma((3, ROWS)),
        ],
        compiler_params=pltpu.CompilerParams(
            collective_id=0, has_side_effects=True, vmem_limit_bytes=60 * 1024 * 1024
        ),
    )(grid, omega.T, legendre_weights, radial_inverses)


def solution(mesh):
    in_specs = (P("row", "ta", None), P("row", "ta"), P("ta", "row", None), P("row", None))
    out_specs = P("ta", "row", None)
    return jax.shard_map(
        functools.partial(shards, mesh.shape["ta"]), mesh=mesh, in_specs=in_specs, out_specs=out_specs, check_vma=False
    )
```

```python
import functools

import jax
import jax.numpy as jnp
from jax import lax
from jax.experimental import pallas as pl
from jax.experimental.pallas import tpu as pltpu
from jax.sharding import PartitionSpec as P

MESH = pl.DeviceIdType.MESH
F32 = jnp.float32
BF16 = jnp.bfloat16
ROWS = 4
LANES = 128


def dot(a, b):
    return jnp.dot(a, b, preferred_element_type=F32)


def iota(shape, dim):
    return lax.broadcasted_iota(jnp.int32, shape, dim)


def one_hot(target, width):
    return jnp.where(target == iota((target.shape[0], width), 1), 1.0, 0.0).astype(BF16)


def kernel(
    tasks, grid_hbm, omega_hbm, weights_hbm, inverses_hbm, out_ref,
    turn, grid_v, omega_ref, omega_v, send, recv, weights, flat_inverses, paired_inverses,
    flip, spread, sym_anti, spec_send, spec_recv, merge, spectra, solved, finish,
    grid_sem, omega_sem, inv_sem, own_sem, send_sem, recv_sem, wsend_sem, wrecv_sem, wrelay_sem, ysend_sem, yrecv_sem,
):
    row = lax.axis_index("row")
    task = lax.axis_index("ta")
    block = tasks
    half_lats = 4 * tasks
    orders = 8 * tasks
    groups = tasks // 4
    diagonal = (4 * task) // block

    def alive(unit, r):
        if unit == 0:
            return True
        return r >= diagonal if unit == 1 else r <= diagonal

    def when(condition):
        return (lambda f: f()) if condition is True else pl.when(condition)

    grid_copy = pltpu.make_async_copy(grid_hbm, grid_v, grid_sem)
    grid_copy.start()
    omega_copy = pltpu.make_async_copy(omega_hbm, omega_ref, omega_sem)
    omega_copy.start()

    barrier = pltpu.get_barrier_semaphore()

    @pl.loop(1, tasks)
    def _(offset):
        pl.semaphore_signal(barrier, 1, device_id={"ta": lax.rem(task + offset, tasks)}, device_id_type=MESH)

    for offset in range(1, ROWS):
        pl.semaphore_signal(barrier, 1, device_id={"row": lax.rem(row + offset, ROWS)}, device_id_type=MESH)


    def unit_source(unit, u):
        slot = 2 * u + (1 if unit == 2 else 0)
        first = 0 if unit == 1 else block
        return weights_hbm.at[slot, pl.ds(first, block), :]

    for unit in range(3):
        for u in range(4):
            pltpu.make_async_copy(unit_source(unit, u), weights.at[unit, row, u], own_sem).start()
    for i in range(32):
        pltpu.make_async_copy(
            inverses_hbm.at[:, pl.ds(i * LANES, LANES)], flat_inverses.at[:, i, :], inv_sem
        ).start()

    source = iota((LANES, LANES), 0)
    target = iota((LANES, LANES), 1)
    sign = jnp.where(target % 2 == 0, 1.0, -1.0)
    turn[...] = jnp.where(source == target + 1 - 2 * (target % 2), sign, 0.0).astype(BF16)
    omega_copy.wait()
    for r in range(16):
        omega_v[pl.ds(8 * r, 8), :] = jnp.broadcast_to(omega_ref[:, r : r + 1], (8, LANES))
    grid_copy.wait()

    lane = iota((1, LANES), 1)
    left_half = lane < 64
    first = (lane // 32) % 2 == 0
    low = (lane // 4) % 2 == 0
    unroll = min(4, groups)

    @pl.loop(0, groups // unroll)
    def _(step):
        for i in range(unroll):
            group = step * unroll + i
            lanes = pl.ds(pl.multiple_of(group * LANES, LANES), LANES)
            values = grid_v[:, :, lanes].astype(F32).reshape(16 * 8, LANES)
            slot = group * 32 + lane // 4
            order = jnp.where(slot % 2 == 0, slot // 2, orders - 1 - slot // 2).astype(F32)
            partner = dot(values.astype(BF16), turn[...])
            forced = values + (omega_v[...] * order) * partner
            t0, t1, t2, t3 = (forced[32 * q : 32 * q + 32].astype(BF16) for q in range(4))
            a0 = jnp.where(left_half, t0, pltpu.roll(t2, 64, 1))
            a2 = jnp.where(left_half, pltpu.roll(t0, 64, 1), t2)
            a1 = jnp.where(left_half, t1, pltpu.roll(t3, 64, 1))
            a3 = jnp.where(left_half, pltpu.roll(t1, 64, 1), t3)
            packed = (
                jnp.where(first, a0, pltpu.roll(a1, 32, 1)),
                jnp.where(first, pltpu.roll(a0, 96, 1), a1),
                jnp.where(first, a2, pltpu.roll(a3, 32, 1)),
                jnp.where(first, pltpu.roll(a2, 96, 1), a3),
            )
            for d in range(4):
                near, far = packed[d][:16], packed[d][16:]
                send[0, group * 4 + d] = jnp.where(low, near, pltpu.roll(far, 4, 1)).astype(BF16)
                send[1, group * 4 + d] = jnp.where(low, pltpu.roll(near, LANES - 4, 1), far).astype(BF16)

    n = half_lats
    flip[...] = one_hot(n - 1 - iota((n, 1), 0), n)
    index = iota((256, 1), 0)
    radius = 4 * ((index // 32) % 4) + 2 * ((index // 4) % 2) + index // LANES
    spread[...] = one_hot(((index // 8) % 4) * 64 + (index % 4) * 16 + radius, 256)
    index = iota((512, 1), 0)
    for second in range(2):
        column = ((index // 16) % 4) * 64 + (index // LANES) * 16 + index % 16
        merge[second] = one_hot(jnp.where((index // 64) % 2 == second, column, -1), 256)
    index = iota((256, 1), 0)
    kind = (index // 32) % 4
    finish[...] = one_hot((2 * (index % 32) + kind % 2) * 4 + (index // LANES) * 2 + kind // 2, 256)
    spectra[...] = jnp.zeros_like(spectra)
    for u in range(4):
        out_ref[2 * u + 1, :block, :] = jnp.zeros((block, 256), BF16)

    pl.semaphore_wait(barrier, tasks - 1 + ROWS - 1)

    pltpu.make_async_copy(weights.at[:, 0], weights.at[:, 0], own_sem).wait()

    def offer(unit):
        @when(alive(unit, row))
        def _():
            for offset in (1, ROWS - 1):
                pltpu.make_async_remote_copy(
                    src_ref=weights.at[unit, row],
                    dst_ref=weights.at[unit, row],
                    send_sem=wsend_sem.at[unit],
                    recv_sem=wrecv_sem.at[offset, unit],
                    device_id={"row": lax.rem(row + offset, ROWS)},
                    device_id_type=MESH,
                ).start()

    offer(0)
    offer(1)

    def deliver(high, to):
        pltpu.make_async_remote_copy(
            src_ref=send.at[high, to],
            dst_ref=recv.at[high, task],
            send_sem=send_sem.at[high],
            recv_sem=recv_sem.at[high],
            device_id={"ta": to},
            device_id_type=MESH,
        ).start()

    planes = max(tasks // 8, 1)
    width = tasks // planes
    plane, place = task // width, task % width
    steps = sorted(range(planes), key=lambda d: -min(d, planes - d))

    for high in range(2):

        @pl.loop(0, width)
        def _(i):
            for d in steps:
                if d > 0:
                    deliver(high, lax.rem(plane + d, planes) * width + lax.rem(place + i, width))

        @pl.loop(1, width)
        def _(i):
            deliver(high, plane * width + lax.rem(place + i, width))

        if high == 0:
            offer(2)

    recv[:, task] = send[:, task]

    pltpu.make_async_copy(flat_inverses, flat_inverses, inv_sem).wait()

    def pair_inverses(start):
        @pl.loop(start // 4, (start + block) // 4)
        def _(step):
            lane = iota((1, LANES), 1)
            turned = flat_inverses[pl.ds(step * 4, 4)].reshape(LANES, LANES).T.astype(BF16)
            for i in range(4):
                even = pltpu.roll(turned[:64], (LANES - 32 * i) % LANES, 1)
                odd = pltpu.roll(turned[64:], (LANES + 32 - 32 * i) % LANES, 1)
                top = jnp.where(lane < 32, even, jnp.where(lane < 64, odd, jnp.zeros_like(odd)))
                paired_inverses[step * 4 + i] = jnp.concatenate([top, pltpu.roll(top, 64, 1)], 0)

    def relay(unit, source, to):
        @when(alive(unit, source))
        def _():
            block_ref = weights.at[unit, source]
            pltpu.make_async_copy(block_ref, block_ref, wrecv_sem.at[1 if unit == 0 else 3, unit]).wait()
            pltpu.make_async_remote_copy(
                src_ref=block_ref,
                dst_ref=block_ref,
                send_sem=wrelay_sem.at[unit],
                recv_sem=wrecv_sem.at[2, unit],
                device_id={"row": to},
                device_id_type=MESH,
            ).start()

    right, left_row, across = (lax.rem(row + i, ROWS) for i in (1, 3, 2))
    pair_inverses(0)
    relay(0, left_row, right)
    relay(1, right, left_row)
    pair_inverses(block)
    relay(2, right, left_row)

    def weights_here(unit):
        for offset, source in ((1, left_row), (2, across), (3, right)):
            if offset != 2 and (offset == 1) == (unit == 0):
                continue

            @when(alive(unit, source))
            def _():
                block_ref = weights.at[unit, source]
                pltpu.make_async_copy(block_ref, block_ref, wrecv_sem.at[offset, unit]).wait()

    def separate(high):
        rest = recv.at[high, pl.ds(0, tasks - 1)]
        pltpu.make_async_copy(rest, rest, recv_sem.at[high]).wait()
        arrived = recv[high].astype(F32)
        halves = [arrived[:, 8 * h : 8 * h + 8, :].reshape(2 * half_lats, LANES) for h in range(2)]
        northern = jnp.concatenate([half[:half_lats] for half in halves], 1)
        southern = jnp.concatenate([half[half_lats:] for half in halves], 1)
        southern = dot(flip[...], southern.astype(BF16))
        for which, part in enumerate((northern + southern, northern - southern)):
            columns = dot(part.astype(BF16), spread[...]).astype(BF16)
            for pair in range(2):
                sym_anti[high, pair, :, pl.ds(which * LANES, LANES)] = columns[:, pair * LANES : (pair + 1) * LANES]

    even_row = iota((4 * block, 1), 0) % 2 == 0
    def transform(unit):
        high = 1 if unit == 2 else 0
        for pair in range(2):
            data = sym_anti[high, pair]
            results = []
            for which in range(2):
                both = dot(weights[unit, :, 2 * pair + which].reshape(4 * block, half_lats), data)
                even_order = (which + high) % 2 == 0
                first, second = both[:, :LANES], both[:, LANES:]
                results.append(jnp.where(even_row, first, second) if even_order else jnp.where(even_row, second, first))
            merged = jnp.where(left_half, results[0], results[1]).astype(BF16)
            spec_send[unit, :, pair] = merged.reshape(4, block, LANES)
        for offset in (2, 1, 3):
            to = lax.rem(row + offset, ROWS)

            @when(alive(unit, to))
            def _():
                pltpu.make_async_remote_copy(
                    src_ref=spec_send.at[unit, to],
                    dst_ref=spec_recv.at[unit, row],
                    send_sem=ysend_sem.at[unit, offset],
                    recv_sem=yrecv_sem.at[unit, offset],
                    device_id={"row": to},
                    device_id_type=MESH,
                ).start()

        spec_recv[unit, row] = spec_send[unit, row]

    weights_here(0)
    weights_here(1)
    separate(0)
    transform(0)
    transform(1)
    weights_here(2)
    separate(1)
    transform(2)

    def arrive(unit):
        @when(alive(unit, row))
        def _():
            for offset in range(1, ROWS):
                source = lax.rem(row + ROWS - offset, ROWS)
                pltpu.make_async_copy(
                    spec_recv.at[unit, source], spec_recv.at[unit, source], yrecv_sem.at[unit, offset]
                ).wait()
            for pair in range(2):
                joined = jnp.concatenate([spec_recv[unit, r, pair] for r in range(ROWS)], 1)
                for second in range(2):
                    spectrum = dot(joined, merge[second])
                    for field in range(2):
                        spot = (2 * pair + second) * 2 + field
                        spectra[unit, pl.ds(spot, block, stride=8), :] = spectrum[:, field * LANES : (field + 1) * LANES]

    def solve(unit):
        arrive(unit)
        start = 0 if unit == 1 else block
        unroll = min(32, block)

        @pl.loop(0, block // unroll)
        def _(step):
            for i in range(unroll):
                k = step * unroll + i
                lhs = spectra[unit, pl.ds(pl.multiple_of(k * 8, 8), 8), :].astype(BF16)
                solved[unit, pl.ds(k, 8, stride=block), :] = dot(lhs, paired_inverses[start + k])

        for u in range(4):
            fields = [solved[unit, pl.ds((2 * u + field) * block, block), :] for field in range(2)]
            result = dot(jnp.concatenate(fields, 1).astype(BF16), finish[...]).astype(BF16)
            out_ref[2 * u + (1 if unit == 2 else 0), pl.ds(start, block), :] = result

    solve(0)
    solve(1)
    solve(2)

    for high in range(2):
        sent = send.at[high, pl.ds(0, tasks - 1)]
        pltpu.make_async_copy(sent, sent, send_sem.at[high]).wait()
    for unit in range(3):

        @when(alive(unit, row))
        def _():
            sent = weights.at[unit, pl.ds(0, 2)]
            pltpu.make_async_copy(sent, sent, wsend_sem.at[unit]).wait()

        @when(alive(unit, left_row if unit == 0 else right))
        def _():
            sent = weights.at[unit, 0]
            pltpu.make_async_copy(sent, sent, wrelay_sem.at[unit]).wait()

        for offset in range(1, ROWS):
            to = lax.rem(row + offset, ROWS)

            @when(alive(unit, to))
            def _():
                sent = spec_send.at[unit, to]
                pltpu.make_async_copy(sent, sent, ysend_sem.at[unit, offset]).wait()


def shards(tasks, grid, omega, legendre_weights, radial_inverses):
    block = tasks
    half_lats = 4 * tasks
    in_hbm = pl.BlockSpec(memory_space=pltpu.HBM)
    in_vmem = pl.BlockSpec(memory_space=pltpu.VMEM)
    dma = pltpu.SemaphoreType.DMA
    return pl.pallas_call(
        functools.partial(kernel, tasks),
        out_shape=jax.ShapeDtypeStruct(legendre_weights.shape[:2] + (256,), BF16),
        in_specs=[in_hbm] * 4,
        out_specs=in_vmem,
        scratch_shapes=[
            pltpu.VMEM((LANES, LANES), BF16),
            pltpu.VMEM((16, 8, 32 * tasks), BF16),
            pltpu.VMEM((8, 16), F32),
            pltpu.VMEM((128, LANES), F32),
            pltpu.VMEM((2, tasks, 16, LANES), BF16),
            pltpu.VMEM((2, tasks, 16, LANES), BF16),
            pltpu.VMEM((3, ROWS, 4, block, half_lats), BF16),
            pltpu.VMEM((2 * block, 32, LANES), F32),
            pltpu.VMEM((2 * block, LANES, LANES), BF16),
            pltpu.VMEM((half_lats, half_lats), BF16),
            pltpu.VMEM((256, 256), BF16),
            pltpu.VMEM((2, 2, half_lats, 256), BF16),
            pltpu.VMEM((3, ROWS, 2, block, LANES), BF16),
            pltpu.VMEM((3, ROWS, 2, block, LANES), BF16),
            pltpu.VMEM((2, 512, 256), BF16),
            pltpu.VMEM((3, block * 8, LANES), F32),
            pltpu.VMEM((3, block * 8, LANES), F32),
            pltpu.VMEM((256, 256), BF16),
            dma, dma, dma, dma, dma((2,)), dma((2,)),
            dma((3,)), dma((ROWS, 3)), dma((3,)), dma((3, ROWS)), dma((3, ROWS)),
        ],
        compiler_params=pltpu.CompilerParams(
            collective_id=0, has_side_effects=True, vmem_limit_bytes=60 * 1024 * 1024
        ),
    )(grid, omega.T, legendre_weights, radial_inverses)


def solution(mesh):
    in_specs = (P("row", "ta", None), P("row", "ta"), P("ta", "row", None), P("row", None))
    out_specs = P("ta", "row", None)
    return jax.shard_map(
        functools.partial(shards, mesh.shape["ta"]), mesh=mesh, in_specs=in_specs, out_specs=out_specs, check_vma=False
    )
```

```python
import functools

import jax
import jax.numpy as jnp
from jax import lax
from jax.experimental import pallas as pl
from jax.experimental.pallas import tpu as pltpu
from jax.sharding import PartitionSpec as P

MESH = pl.DeviceIdType.MESH
F32 = jnp.float32
BF16 = jnp.bfloat16
ROWS = 4
LANES = 128


def dot(a, b):
    return jnp.dot(a, b, preferred_element_type=F32)


def iota(shape, dim):
    return lax.broadcasted_iota(jnp.int32, shape, dim)


def one_hot(target, width):
    return jnp.where(target == iota((target.shape[0], width), 1), 1.0, 0.0).astype(BF16)


def kernel(
    tasks, grid_hbm, omega_hbm, weights_hbm, inverses_hbm, out_ref,
    turn, grid_v, omega_ref, omega_v, send, recv, weights, flat_inverses, paired_inverses,
    flip, spread, sym_anti, spec_send, spec_recv, merge, spectra, solved, finish,
    grid_sem, omega_sem, inv_sem, own_sem, send_sem, recv_sem, wsend_sem, wrecv_sem, wrelay_sem, ysend_sem, yrecv_sem,
):
    row = lax.axis_index("row")
    task = lax.axis_index("ta")
    block = tasks
    half_lats = 4 * tasks
    orders = 8 * tasks
    groups = tasks // 4
    diagonal = (4 * task) // block

    def alive(unit, r):
        if unit == 0:
            return True
        return r >= diagonal if unit == 1 else r <= diagonal

    def when(condition):
        return (lambda f: f()) if condition is True else pl.when(condition)

    grid_copy = pltpu.make_async_copy(grid_hbm, grid_v, grid_sem)
    grid_copy.start()
    omega_copy = pltpu.make_async_copy(omega_hbm, omega_ref, omega_sem)
    omega_copy.start()

    barrier = pltpu.get_barrier_semaphore()

    @pl.loop(1, tasks)
    def _(offset):
        pl.semaphore_signal(barrier, 1, device_id={"ta": lax.rem(task + offset, tasks)}, device_id_type=MESH)

    for offset in range(1, ROWS):
        pl.semaphore_signal(barrier, 1, device_id={"row": lax.rem(row + offset, ROWS)}, device_id_type=MESH)


    def unit_source(unit, u):
        slot = 2 * u + (1 if unit == 2 else 0)
        first = 0 if unit == 1 else block
        return weights_hbm.at[slot, pl.ds(first, block), :]

    for unit in range(3):
        for u in range(4):
            pltpu.make_async_copy(unit_source(unit, u), weights.at[unit, row, u], own_sem).start()
    for i in range(32):
        pltpu.make_async_copy(
            inverses_hbm.at[:, pl.ds(i * LANES, LANES)], flat_inverses.at[:, i, :], inv_sem
        ).start()

    source = iota((LANES, LANES), 0)
    target = iota((LANES, LANES), 1)
    sign = jnp.where(target % 2 == 0, 1.0, -1.0)
    turn[...] = jnp.where(source == target + 1 - 2 * (target % 2), sign, 0.0).astype(BF16)
    omega_copy.wait()
    for r in range(16):
        omega_v[pl.ds(8 * r, 8), :] = jnp.broadcast_to(omega_ref[:, r : r + 1], (8, LANES))
    grid_copy.wait()

    lane = iota((1, LANES), 1)
    left_half = lane < 64
    first = (lane // 32) % 2 == 0
    low = (lane // 4) % 2 == 0
    unroll = min(4, groups)

    @pl.loop(0, groups // unroll)
    def _(step):
        for i in range(unroll):
            group = step * unroll + i
            lanes = pl.ds(pl.multiple_of(group * LANES, LANES), LANES)
            values = grid_v[:, :, lanes].astype(F32).reshape(16 * 8, LANES)
            slot = group * 32 + lane // 4
            order = jnp.where(slot % 2 == 0, slot // 2, orders - 1 - slot // 2).astype(F32)
            partner = dot(values.astype(BF16), turn[...])
            forced = values + (omega_v[...] * order) * partner
            t0, t1, t2, t3 = (forced[32 * q : 32 * q + 32].astype(BF16) for q in range(4))
            a0 = jnp.where(left_half, t0, pltpu.roll(t2, 64, 1))
            a2 = jnp.where(left_half, pltpu.roll(t0, 64, 1), t2)
            a1 = jnp.where(left_half, t1, pltpu.roll(t3, 64, 1))
            a3 = jnp.where(left_half, pltpu.roll(t1, 64, 1), t3)
            packed = (
                jnp.where(first, a0, pltpu.roll(a1, 32, 1)),
                jnp.where(first, pltpu.roll(a0, 96, 1), a1),
                jnp.where(first, a2, pltpu.roll(a3, 32, 1)),
                jnp.where(first, pltpu.roll(a2, 96, 1), a3),
            )
            for d in range(4):
                near, far = packed[d][:16], packed[d][16:]
                send[0, group * 4 + d] = jnp.where(low, near, pltpu.roll(far, 4, 1)).astype(BF16)
                send[1, group * 4 + d] = jnp.where(low, pltpu.roll(near, LANES - 4, 1), far).astype(BF16)

    n = half_lats
    flip[...] = one_hot(n - 1 - iota((n, 1), 0), n)
    index = iota((256, 1), 0)
    radius = 4 * ((index // 32) % 4) + 2 * ((index // 4) % 2) + index // LANES
    spread[...] = one_hot(((index // 8) % 4) * 64 + (index % 4) * 16 + radius, 256)
    index = iota((512, 1), 0)
    for second in range(2):
        column = ((index // 16) % 4) * 64 + (index // LANES) * 16 + index % 16
        merge[second] = one_hot(jnp.where((index // 64) % 2 == second, column, -1), 256)
    index = iota((256, 1), 0)
    kind = (index // 32) % 4
    finish[...] = one_hot((2 * (index % 32) + kind % 2) * 4 + (index // LANES) * 2 + kind // 2, 256)
    spectra[...] = jnp.zeros_like(spectra)
    for u in range(4):
        out_ref[2 * u + 1, :block, :] = jnp.zeros((block, 256), BF16)

    pl.semaphore_wait(barrier, tasks - 1 + ROWS - 1)

    pltpu.make_async_copy(weights.at[:, 0], weights.at[:, 0], own_sem).wait()

    def offer(unit):
        @when(alive(unit, row))
        def _():
            for offset in (1, ROWS - 1):
                pltpu.make_async_remote_copy(
                    src_ref=weights.at[unit, row],
                    dst_ref=weights.at[unit, row],
                    send_sem=wsend_sem.at[unit],
                    recv_sem=wrecv_sem.at[offset, unit],
                    device_id={"row": lax.rem(row + offset, ROWS)},
                    device_id_type=MESH,
                ).start()

    offer(0)
    offer(1)

    def deliver(high, to):
        pltpu.make_async_remote_copy(
            src_ref=send.at[high, to],
            dst_ref=recv.at[high, task],
            send_sem=send_sem.at[high],
            recv_sem=recv_sem.at[high],
            device_id={"ta": to},
            device_id_type=MESH,
        ).start()

    planes = max(tasks // 8, 1)
    width = tasks // planes
    plane, place = task // width, task % width
    steps = sorted(range(planes), key=lambda d: -min(d, planes - d))

    for high in range(2):

        @pl.loop(0, width)
        def _(i):
            for d in steps:
                if d > 0:
                    deliver(high, lax.rem(plane + d, planes) * width + lax.rem(place + i, width))

        @pl.loop(1, width)
        def _(i):
            deliver(high, plane * width + lax.rem(place + i, width))

        if high == 0:
            offer(2)

    recv[:, task] = send[:, task]

    pltpu.make_async_copy(flat_inverses, flat_inverses, inv_sem).wait()

    def pair_inverses(start):
        @pl.loop(start // 4, (start + block) // 4)
        def _(step):
            lane = iota((1, LANES), 1)
            turned = flat_inverses[pl.ds(step * 4, 4)].reshape(LANES, LANES).T.astype(BF16)
            even = [turned[:64] if r == 0 else pltpu.roll(turned[:64], 32 * r, 1) for r in range(4)]
            odd = [turned[64:] if r == 0 else pltpu.roll(turned[64:], 32 * r, 1) for r in range(4)]
            zero = jnp.zeros_like(turned[:64])
            for i in range(4):
                top = jnp.where(lane < 32, even[-i % 4], jnp.where(lane < 64, odd[(1 - i) % 4], zero))
                bottom = jnp.where(lane < 64, zero, jnp.where(lane < 96, even[(2 - i) % 4], odd[(3 - i) % 4]))
                paired_inverses[step * 4 + i] = jnp.concatenate([top, bottom], 0)

    def relay(unit, source, to):
        @when(alive(unit, source))
        def _():
            block_ref = weights.at[unit, source]
            pltpu.make_async_copy(block_ref, block_ref, wrecv_sem.at[1 if unit == 0 else 3, unit]).wait()
            pltpu.make_async_remote_copy(
                src_ref=block_ref,
                dst_ref=block_ref,
                send_sem=wrelay_sem.at[unit],
                recv_sem=wrecv_sem.at[2, unit],
                device_id={"row": to},
                device_id_type=MESH,
            ).start()

    right, left_row, across = (lax.rem(row + i, ROWS) for i in (1, 3, 2))
    pair_inverses(0)
    relay(0, left_row, right)
    relay(1, right, left_row)
    pair_inverses(block)
    relay(2, right, left_row)

    def weights_here(unit):
        for offset, source in ((1, left_row), (2, across), (3, right)):
            if offset != 2 and (offset == 1) == (unit == 0):
                continue

            @when(alive(unit, source))
            def _():
                block_ref = weights.at[unit, source]
                pltpu.make_async_copy(block_ref, block_ref, wrecv_sem.at[offset, unit]).wait()

    def separate(high):
        rest = recv.at[high, pl.ds(0, tasks - 1)]
        pltpu.make_async_copy(rest, rest, recv_sem.at[high]).wait()
        arrived = recv[high].astype(F32)
        halves = [arrived[:, 8 * h : 8 * h + 8, :].reshape(2 * half_lats, LANES) for h in range(2)]
        northern = jnp.concatenate([half[:half_lats] for half in halves], 1)
        southern = jnp.concatenate([half[half_lats:] for half in halves], 1)
        southern = dot(flip[...], southern.astype(BF16))
        for which, part in enumerate((northern + southern, northern - southern)):
            columns = dot(part.astype(BF16), spread[...]).astype(BF16)
            for pair in range(2):
                sym_anti[high, pair, :, pl.ds(which * LANES, LANES)] = columns[:, pair * LANES : (pair + 1) * LANES]

    even_row = iota((4 * block, 1), 0) % 2 == 0
    def transform(unit):
        high = 1 if unit == 2 else 0
        for pair in range(2):
            data = sym_anti[high, pair]
            results = []
            for which in range(2):
                both = dot(weights[unit, :, 2 * pair + which].reshape(4 * block, half_lats), data)
                even_order = (which + high) % 2 == 0
                first, second = both[:, :LANES], both[:, LANES:]
                results.append(jnp.where(even_row, first, second) if even_order else jnp.where(even_row, second, first))
            merged = jnp.where(left_half, results[0], results[1]).astype(BF16)
            spec_send[unit, :, pair] = merged.reshape(4, block, LANES)
        for offset in (2, 1, 3):
            to = lax.rem(row + offset, ROWS)

            @when(alive(unit, to))
            def _():
                pltpu.make_async_remote_copy(
                    src_ref=spec_send.at[unit, to],
                    dst_ref=spec_recv.at[unit, row],
                    send_sem=ysend_sem.at[unit, offset],
                    recv_sem=yrecv_sem.at[unit, offset],
                    device_id={"row": to},
                    device_id_type=MESH,
                ).start()

        spec_recv[unit, row] = spec_send[unit, row]

    weights_here(0)
    weights_here(1)
    separate(0)
    transform(0)
    transform(1)
    weights_here(2)
    separate(1)
    transform(2)

    def arrive(unit):
        @when(alive(unit, row))
        def _():
            for offset in range(1, ROWS):
                source = lax.rem(row + ROWS - offset, ROWS)
                pltpu.make_async_copy(
                    spec_recv.at[unit, source], spec_recv.at[unit, source], yrecv_sem.at[unit, offset]
                ).wait()
            for pair in range(2):
                joined = jnp.concatenate([spec_recv[unit, r, pair] for r in range(ROWS)], 1)
                for second in range(2):
                    spectrum = dot(joined, merge[second])
                    for field in range(2):
                        spot = (2 * pair + second) * 2 + field
                        spectra[unit, pl.ds(spot, block, stride=8), :] = spectrum[:, field * LANES : (field + 1) * LANES]

    def solve(unit):
        arrive(unit)
        start = 0 if unit == 1 else block
        unroll = min(64, block)

        @pl.loop(0, block // unroll)
        def _(step):
            for i in range(unroll):
                k = step * unroll + i
                lhs = spectra[unit, pl.ds(pl.multiple_of(k * 8, 8), 8), :].astype(BF16)
                solved[unit, pl.ds(k, 8, stride=block), :] = dot(lhs, paired_inverses[start + k])

        for u in range(4):
            fields = [solved[unit, pl.ds((2 * u + field) * block, block), :] for field in range(2)]
            result = dot(jnp.concatenate(fields, 1).astype(BF16), finish[...]).astype(BF16)
            out_ref[2 * u + (1 if unit == 2 else 0), pl.ds(start, block), :] = result

    solve(0)
    solve(1)
    solve(2)

    for high in range(2):
        sent = send.at[high, pl.ds(0, tasks - 1)]
        pltpu.make_async_copy(sent, sent, send_sem.at[high]).wait()
    for unit in range(3):

        @when(alive(unit, row))
        def _():
            sent = weights.at[unit, pl.ds(0, 2)]
            pltpu.make_async_copy(sent, sent, wsend_sem.at[unit]).wait()

        @when(alive(unit, left_row if unit == 0 else right))
        def _():
            sent = weights.at[unit, 0]
            pltpu.make_async_copy(sent, sent, wrelay_sem.at[unit]).wait()

        for offset in range(1, ROWS):
            to = lax.rem(row + offset, ROWS)

            @when(alive(unit, to))
            def _():
                sent = spec_send.at[unit, to]
                pltpu.make_async_copy(sent, sent, ysend_sem.at[unit, offset]).wait()


def shards(tasks, grid, omega, legendre_weights, radial_inverses):
    block = tasks
    half_lats = 4 * tasks
    in_hbm = pl.BlockSpec(memory_space=pltpu.HBM)
    in_vmem = pl.BlockSpec(memory_space=pltpu.VMEM)
    dma = pltpu.SemaphoreType.DMA
    return pl.pallas_call(
        functools.partial(kernel, tasks),
        out_shape=jax.ShapeDtypeStruct(legendre_weights.shape[:2] + (256,), BF16),
        in_specs=[in_hbm] * 4,
        out_specs=in_vmem,
        scratch_shapes=[
            pltpu.VMEM((LANES, LANES), BF16),
            pltpu.VMEM((16, 8, 32 * tasks), BF16),
            pltpu.VMEM((8, 16), F32),
            pltpu.VMEM((128, LANES), F32),
            pltpu.VMEM((2, tasks, 16, LANES), BF16),
            pltpu.VMEM((2, tasks, 16, LANES), BF16),
            pltpu.VMEM((3, ROWS, 4, block, half_lats), BF16),
            pltpu.VMEM((2 * block, 32, LANES), F32),
            pltpu.VMEM((2 * block, LANES, LANES), BF16),
            pltpu.VMEM((half_lats, half_lats), BF16),
            pltpu.VMEM((256, 256), BF16),
            pltpu.VMEM((2, 2, half_lats, 256), BF16),
            pltpu.VMEM((3, ROWS, 2, block, LANES), BF16),
            pltpu.VMEM((3, ROWS, 2, block, LANES), BF16),
            pltpu.VMEM((2, 512, 256), BF16),
            pltpu.VMEM((3, block * 8, LANES), F32),
            pltpu.VMEM((3, block * 8, LANES), F32),
            pltpu.VMEM((256, 256), BF16),
            dma, dma, dma, dma, dma((2,)), dma((2,)),
            dma((3,)), dma((ROWS, 3)), dma((3,)), dma((3, ROWS)), dma((3, ROWS)),
        ],
        compiler_params=pltpu.CompilerParams(
            collective_id=0, has_side_effects=True, vmem_limit_bytes=60 * 1024 * 1024
        ),
    )(grid, omega.T, legendre_weights, radial_inverses)


def solution(mesh):
    in_specs = (P("row", "ta", None), P("row", "ta"), P("ta", "row", None), P("row", None))
    out_specs = P("ta", "row", None)
    return jax.shard_map(
        functools.partial(shards, mesh.shape["ta"]), mesh=mesh, in_specs=in_specs, out_specs=out_specs, check_vma=False
    )
```

```python
import functools

import jax
import jax.numpy as jnp
from jax import lax
from jax.experimental import pallas as pl
from jax.experimental.pallas import tpu as pltpu
from jax.sharding import PartitionSpec as P

MESH = pl.DeviceIdType.MESH
F32 = jnp.float32
BF16 = jnp.bfloat16
ROWS = 4
LANES = 128


def dot(a, b):
    return jnp.dot(a, b, preferred_element_type=F32)


def iota(shape, dim):
    return lax.broadcasted_iota(jnp.int32, shape, dim)


def one_hot(target, width):
    return jnp.where(target == iota((target.shape[0], width), 1), 1.0, 0.0).astype(BF16)


def kernel(
    tasks, grid_hbm, omega_hbm, weights_hbm, inverses_hbm, out_ref,
    turn, grid_v, omega_ref, omega_v, send, recv, weights, flat_inverses, paired_inverses,
    flip, spread, sym_anti, spec_send, spec_recv, merge, spectra, solved, finish,
    grid_sem, omega_sem, inv_sem, own_sem, send_sem, recv_sem, wsend_sem, wrecv_sem, wrelay_sem, ysend_sem, yrecv_sem,
):
    row = lax.axis_index("row")
    task = lax.axis_index("ta")
    block = tasks
    half_lats = 4 * tasks
    orders = 8 * tasks
    groups = tasks // 4
    diagonal = (4 * task) // block

    def alive(unit, r):
        if unit == 0:
            return True
        return r >= diagonal if unit == 1 else r <= diagonal

    def when(condition):
        return (lambda f: f()) if condition is True else pl.when(condition)

    grid_copy = pltpu.make_async_copy(grid_hbm, grid_v, grid_sem)
    grid_copy.start()
    omega_copy = pltpu.make_async_copy(omega_hbm, omega_ref, omega_sem)
    omega_copy.start()

    barrier = pltpu.get_barrier_semaphore()

    @pl.loop(1, tasks)
    def _(offset):
        pl.semaphore_signal(barrier, 1, device_id={"ta": lax.rem(task + offset, tasks)}, device_id_type=MESH)

    for offset in range(1, ROWS):
        pl.semaphore_signal(barrier, 1, device_id={"row": lax.rem(row + offset, ROWS)}, device_id_type=MESH)


    def unit_source(unit, u):
        slot = 2 * u + (1 if unit == 2 else 0)
        first = 0 if unit == 1 else block
        return weights_hbm.at[slot, pl.ds(first, block), :]

    for unit in range(3):
        for u in range(4):
            pltpu.make_async_copy(unit_source(unit, u), weights.at[unit, row, u], own_sem).start()
    for i in range(32):
        pltpu.make_async_copy(
            inverses_hbm.at[:, pl.ds(i * LANES, LANES)], flat_inverses.at[:, i, :], inv_sem
        ).start()

    source = iota((LANES, LANES), 0)
    target = iota((LANES, LANES), 1)
    sign = jnp.where(target % 2 == 0, 1.0, -1.0)
    turn[...] = jnp.where(source == target + 1 - 2 * (target % 2), sign, 0.0).astype(BF16)
    omega_copy.wait()
    for r in range(16):
        omega_v[pl.ds(8 * r, 8), :] = jnp.broadcast_to(omega_ref[:, r : r + 1], (8, LANES))
    grid_copy.wait()

    lane = iota((1, LANES), 1)
    left_half = lane < 64
    first = (lane // 32) % 2 == 0
    low = (lane // 4) % 2 == 0
    unroll = min(4, groups)

    @pl.loop(0, groups // unroll)
    def _(step):
        for i in range(unroll):
            group = step * unroll + i
            lanes = pl.ds(pl.multiple_of(group * LANES, LANES), LANES)
            values = grid_v[:, :, lanes].astype(F32).reshape(16 * 8, LANES)
            slot = group * 32 + lane // 4
            order = jnp.where(slot % 2 == 0, slot // 2, orders - 1 - slot // 2).astype(F32)
            partner = dot(values.astype(BF16), turn[...])
            forced = values + (omega_v[...] * order) * partner
            t0, t1, t2, t3 = (forced[32 * q : 32 * q + 32].astype(BF16) for q in range(4))
            a0 = jnp.where(left_half, t0, pltpu.roll(t2, 64, 1))
            a2 = jnp.where(left_half, pltpu.roll(t0, 64, 1), t2)
            a1 = jnp.where(left_half, t1, pltpu.roll(t3, 64, 1))
            a3 = jnp.where(left_half, pltpu.roll(t1, 64, 1), t3)
            packed = (
                jnp.where(first, a0, pltpu.roll(a1, 32, 1)),
                jnp.where(first, pltpu.roll(a0, 96, 1), a1),
                jnp.where(first, a2, pltpu.roll(a3, 32, 1)),
                jnp.where(first, pltpu.roll(a2, 96, 1), a3),
            )
            for d in range(4):
                near, far = packed[d][:16], packed[d][16:]
                send[0, group * 4 + d] = jnp.where(low, near, pltpu.roll(far, 4, 1)).astype(BF16)
                send[1, group * 4 + d] = jnp.where(low, pltpu.roll(near, LANES - 4, 1), far).astype(BF16)

    n = half_lats
    flip[...] = one_hot(n - 1 - iota((n, 1), 0), n)
    index = iota((256, 1), 0)
    radius = 4 * ((index // 32) % 4) + 2 * ((index // 4) % 2) + index // LANES
    spread[...] = one_hot(((index // 8) % 4) * 64 + (index % 4) * 16 + radius, 256)
    index = iota((512, 1), 0)
    for second in range(2):
        column = ((index // 16) % 4) * 64 + (index // LANES) * 16 + index % 16
        merge[second] = one_hot(jnp.where((index // 64) % 2 == second, column, -1), 256)
    index = iota((256, 1), 0)
    kind = (index // 32) % 4
    finish[...] = one_hot((2 * (index % 32) + kind % 2) * 4 + (index // LANES) * 2 + kind // 2, 256)
    spectra[...] = jnp.zeros_like(spectra)
    for u in range(4):
        out_ref[2 * u + 1, :block, :] = jnp.zeros((block, 256), BF16)

    pl.semaphore_wait(barrier, tasks - 1 + ROWS - 1)

    pltpu.make_async_copy(weights.at[:, 0], weights.at[:, 0], own_sem).wait()

    def offer(unit):
        @when(alive(unit, row))
        def _():
            for offset in (1, ROWS - 1):
                pltpu.make_async_remote_copy(
                    src_ref=weights.at[unit, row],
                    dst_ref=weights.at[unit, row],
                    send_sem=wsend_sem.at[unit],
                    recv_sem=wrecv_sem.at[offset, unit],
                    device_id={"row": lax.rem(row + offset, ROWS)},
                    device_id_type=MESH,
                ).start()

    offer(0)
    offer(1)

    def deliver(high, to):
        pltpu.make_async_remote_copy(
            src_ref=send.at[high, to],
            dst_ref=recv.at[high, task],
            send_sem=send_sem.at[high],
            recv_sem=recv_sem.at[high],
            device_id={"ta": to},
            device_id_type=MESH,
        ).start()

    planes = max(tasks // 8, 1)
    width = tasks // planes
    plane, place = task // width, task % width
    steps = sorted(range(planes), key=lambda d: -min(d, planes - d))

    for high in range(2):

        @pl.loop(0, width)
        def _(i):
            for d in steps:
                if d > 0:
                    deliver(high, lax.rem(plane + d, planes) * width + lax.rem(place + i, width))

        @pl.loop(1, width)
        def _(i):
            deliver(high, plane * width + lax.rem(place + i, width))

        if high == 0:
            offer(2)

    recv[:, task] = send[:, task]

    pltpu.make_async_copy(flat_inverses, flat_inverses, inv_sem).wait()

    def pair_inverses(start):
        @pl.loop(start // 4, (start + block) // 4)
        def _(step):
            lane = iota((1, LANES), 1)
            turned = flat_inverses[pl.ds(step * 4, 4)].reshape(LANES, LANES).T.astype(BF16)
            even = [turned[:64] if r == 0 else pltpu.roll(turned[:64], 32 * r, 1) for r in range(4)]
            odd = [turned[64:] if r == 0 else pltpu.roll(turned[64:], 32 * r, 1) for r in range(4)]
            zero = jnp.zeros_like(turned[:64])
            for i in range(4):
                top = jnp.where(lane < 32, even[-i % 4], jnp.where(lane < 64, odd[(1 - i) % 4], zero))
                bottom = jnp.where(lane < 64, zero, jnp.where(lane < 96, even[(2 - i) % 4], odd[(3 - i) % 4]))
                paired_inverses[step * 4 + i] = jnp.concatenate([top, bottom], 0)

    def relay(unit, source, to):
        @when(alive(unit, source))
        def _():
            block_ref = weights.at[unit, source]
            pltpu.make_async_copy(block_ref, block_ref, wrecv_sem.at[1 if unit == 0 else 3, unit]).wait()
            pltpu.make_async_remote_copy(
                src_ref=block_ref,
                dst_ref=block_ref,
                send_sem=wrelay_sem.at[unit],
                recv_sem=wrecv_sem.at[2, unit],
                device_id={"row": to},
                device_id_type=MESH,
            ).start()

    right, left_row, across = (lax.rem(row + i, ROWS) for i in (1, 3, 2))
    pair_inverses(0)
    relay(0, left_row, right)
    relay(1, right, left_row)
    pair_inverses(block)
    relay(2, right, left_row)

    def weights_here(unit):
        for offset, source in ((1, left_row), (2, across), (3, right)):
            if offset != 2 and (offset == 1) == (unit == 0):
                continue

            @when(alive(unit, source))
            def _():
                block_ref = weights.at[unit, source]
                pltpu.make_async_copy(block_ref, block_ref, wrecv_sem.at[offset, unit]).wait()

    def separate(high):
        rest = recv.at[high, pl.ds(0, tasks - 1)]
        pltpu.make_async_copy(rest, rest, recv_sem.at[high]).wait()
        arrived = recv[high].astype(F32)
        halves = [arrived[:, 8 * h : 8 * h + 8, :].reshape(2 * half_lats, LANES) for h in range(2)]
        northern = jnp.concatenate([half[:half_lats] for half in halves], 1)
        southern = jnp.concatenate([half[half_lats:] for half in halves], 1)
        southern = dot(flip[...], southern.astype(BF16))
        for which, part in enumerate((northern + southern, northern - southern)):
            columns = dot(part.astype(BF16), spread[...]).astype(BF16)
            for pair in range(2):
                sym_anti[high, pair, :, pl.ds(which * LANES, LANES)] = columns[:, pair * LANES : (pair + 1) * LANES]

    even_row = iota((4 * block, 1), 0) % 2 == 0
    def transform(unit):
        high = 1 if unit == 2 else 0
        for pair in range(2):
            data = sym_anti[high, pair]
            results = []
            for which in range(2):
                both = dot(weights[unit, :, 2 * pair + which].reshape(4 * block, half_lats), data)
                even_order = (which + high) % 2 == 0
                first, second = both[:, :LANES], both[:, LANES:]
                results.append(jnp.where(even_row, first, second) if even_order else jnp.where(even_row, second, first))
            merged = jnp.where(left_half, results[0], results[1]).astype(BF16)
            spec_send[unit, :, pair] = merged.reshape(4, block, LANES)
        for offset in (2, 1, 3):
            to = lax.rem(row + offset, ROWS)

            @when(alive(unit, to))
            def _():
                pltpu.make_async_remote_copy(
                    src_ref=spec_send.at[unit, to],
                    dst_ref=spec_recv.at[unit, row],
                    send_sem=ysend_sem.at[unit, offset],
                    recv_sem=yrecv_sem.at[unit, offset],
                    device_id={"row": to},
                    device_id_type=MESH,
                ).start()

        spec_recv[unit, row] = spec_send[unit, row]

    weights_here(0)
    weights_here(1)
    separate(0)
    transform(0)
    transform(1)
    weights_here(2)
    separate(1)
    transform(2)

    def arrive(unit):
        @when(alive(unit, row))
        def _():
            for offset in range(1, ROWS):
                source = lax.rem(row + ROWS - offset, ROWS)
                pltpu.make_async_copy(
                    spec_recv.at[unit, source], spec_recv.at[unit, source], yrecv_sem.at[unit, offset]
                ).wait()
            for pair in range(2):
                joined = jnp.concatenate([spec_recv[unit, r, pair] for r in range(ROWS)], 1)
                for second in range(2):
                    spectrum = dot(joined, merge[second])
                    for field in range(2):
                        spot = (2 * pair + second) * 2 + field
                        spectra[unit, pl.ds(spot, block, stride=8), :] = spectrum[:, field * LANES : (field + 1) * LANES]

    def solve(unit):
        arrive(unit)
        start = 0 if unit == 1 else block
        unroll = min(64, block)

        @pl.loop(0, block // unroll)
        def _(step):
            for i in range(unroll):
                k = step * unroll + i
                lhs = spectra[unit, pl.ds(pl.multiple_of(k * 8, 8), 8), :].astype(BF16)
                solved[unit, pl.ds(k, 8, stride=block), :] = dot(lhs, paired_inverses[start + k])

        for u in range(4):
            fields = [solved[unit, pl.ds((2 * u + field) * block, block), :] for field in range(2)]
            result = dot(jnp.concatenate(fields, 1).astype(BF16), finish[...]).astype(BF16)
            out_ref[2 * u + (1 if unit == 2 else 0), pl.ds(start, block), :] = result

    solve(0)
    solve(1)
    solve(2)

    for high in range(2):
        sent = send.at[high, pl.ds(0, tasks - 1)]
        pltpu.make_async_copy(sent, sent, send_sem.at[high]).wait()
    for unit in range(3):

        @when(alive(unit, row))
        def _():
            sent = weights.at[unit, pl.ds(0, 2)]
            pltpu.make_async_copy(sent, sent, wsend_sem.at[unit]).wait()

        @when(alive(unit, left_row if unit == 0 else right))
        def _():
            sent = weights.at[unit, 0]
            pltpu.make_async_copy(sent, sent, wrelay_sem.at[unit]).wait()

        for offset in range(1, ROWS):
            to = lax.rem(row + offset, ROWS)

            @when(alive(unit, to))
            def _():
                sent = spec_send.at[unit, to]
                pltpu.make_async_copy(sent, sent, ysend_sem.at[unit, offset]).wait()


def shards(tasks, grid, omega, legendre_weights, radial_inverses):
    block = tasks
    half_lats = 4 * tasks
    in_hbm = pl.BlockSpec(memory_space=pltpu.HBM)
    in_vmem = pl.BlockSpec(memory_space=pltpu.VMEM)
    dma = pltpu.SemaphoreType.DMA
    return pl.pallas_call(
        functools.partial(kernel, tasks),
        out_shape=jax.ShapeDtypeStruct(legendre_weights.shape[:2] + (256,), BF16),
        in_specs=[in_hbm] * 4,
        out_specs=in_vmem,
        scratch_shapes=[
            pltpu.VMEM((LANES, LANES), BF16),
            pltpu.VMEM((16, 8, 32 * tasks), BF16),
            pltpu.VMEM((8, 16), F32),
            pltpu.VMEM((128, LANES), F32),
            pltpu.VMEM((2, tasks, 16, LANES), BF16),
            pltpu.VMEM((2, tasks, 16, LANES), BF16),
            pltpu.VMEM((3, ROWS, 4, block, half_lats), BF16),
            pltpu.VMEM((2 * block, 32, LANES), F32),
            pltpu.VMEM((2 * block, LANES, LANES), BF16),
            pltpu.VMEM((half_lats, half_lats), BF16),
            pltpu.VMEM((256, 256), BF16),
            pltpu.VMEM((2, 2, half_lats, 256), BF16),
            pltpu.VMEM((3, ROWS, 2, block, LANES), BF16),
            pltpu.VMEM((3, ROWS, 2, block, LANES), BF16),
            pltpu.VMEM((2, 512, 256), BF16),
            pltpu.VMEM((3, block * 8 + 8, LANES), F32),
            pltpu.VMEM((3, block * 9, LANES), F32),
            pltpu.VMEM((256, 256), BF16),
            dma, dma, dma, dma, dma((2,)), dma((2,)),
            dma((3,)), dma((ROWS, 3)), dma((3,)), dma((3, ROWS)), dma((3, ROWS)),
        ],
        compiler_params=pltpu.CompilerParams(
            collective_id=0, has_side_effects=True, vmem_limit_bytes=60 * 1024 * 1024
        ),
    )(grid, omega.T, legendre_weights, radial_inverses)


def solution(mesh):
    in_specs = (P("row", "ta", None), P("row", "ta"), P("ta", "row", None), P("row", None))
    out_specs = P("ta", "row", None)
    return jax.shard_map(
        functools.partial(shards, mesh.shape["ta"]), mesh=mesh, in_specs=in_specs, out_specs=out_specs, check_vma=False
    )
```

```python
import functools

import jax
import jax.numpy as jnp
from jax import lax
from jax.experimental import pallas as pl
from jax.experimental.pallas import tpu as pltpu
from jax.sharding import PartitionSpec as P

MESH = pl.DeviceIdType.MESH
F32 = jnp.float32
BF16 = jnp.bfloat16
ROWS = 4
LANES = 128


def dot(a, b):
    return jnp.dot(a, b, preferred_element_type=F32)


def iota(shape, dim):
    return lax.broadcasted_iota(jnp.int32, shape, dim)


def one_hot(target, width):
    return jnp.where(target == iota((target.shape[0], width), 1), 1.0, 0.0).astype(BF16)


def kernel(
    tasks, grid_hbm, omega_hbm, weights_hbm, inverses_hbm, out_ref,
    turn, grid_v, omega_ref, omega_v, send, recv, weights, flat_inverses, paired_inverses,
    flip, spread, sym_anti, spec_send, spec_recv, merge, spectra, solved, finish,
    grid_sem, omega_sem, inv_sem, own_sem, send_sem, recv_sem, wsend_sem, wrecv_sem, wrelay_sem, ysend_sem, yrecv_sem,
):
    row = lax.axis_index("row")
    task = lax.axis_index("ta")
    block = tasks
    half_lats = 4 * tasks
    orders = 8 * tasks
    groups = tasks // 4
    diagonal = (4 * task) // block

    def alive(unit, r):
        if unit == 0:
            return True
        return r >= diagonal if unit == 1 else r <= diagonal

    def when(condition):
        return (lambda f: f()) if condition is True else pl.when(condition)

    grid_copy = pltpu.make_async_copy(grid_hbm, grid_v, grid_sem)
    grid_copy.start()
    omega_copy = pltpu.make_async_copy(omega_hbm, omega_ref, omega_sem)
    omega_copy.start()

    barrier = pltpu.get_barrier_semaphore()

    @pl.loop(1, tasks)
    def _(offset):
        pl.semaphore_signal(barrier, 1, device_id={"ta": lax.rem(task + offset, tasks)}, device_id_type=MESH)

    for offset in range(1, ROWS):
        pl.semaphore_signal(barrier, 1, device_id={"row": lax.rem(row + offset, ROWS)}, device_id_type=MESH)


    def unit_source(unit, u):
        slot = 2 * u + (1 if unit == 2 else 0)
        first = 0 if unit == 1 else block
        return weights_hbm.at[slot, pl.ds(first, block), :]

    for unit in range(3):
        for u in range(4):
            pltpu.make_async_copy(unit_source(unit, u), weights.at[unit, row, u], own_sem).start()
    for i in range(32):
        pltpu.make_async_copy(
            inverses_hbm.at[:, pl.ds(i * LANES, LANES)], flat_inverses.at[:, i, :], inv_sem
        ).start()

    source = iota((LANES, LANES), 0)
    target = iota((LANES, LANES), 1)
    sign = jnp.where(target % 2 == 0, 1.0, -1.0)
    turn[...] = jnp.where(source == target + 1 - 2 * (target % 2), sign, 0.0).astype(BF16)
    omega_copy.wait()
    for r in range(16):
        omega_v[pl.ds(8 * r, 8), :] = jnp.broadcast_to(omega_ref[:, r : r + 1], (8, LANES))
    grid_copy.wait()

    lane = iota((1, LANES), 1)
    left_half = lane < 64
    first = (lane // 32) % 2 == 0
    low = (lane // 4) % 2 == 0
    unroll = min(4, groups)

    @pl.loop(0, groups // unroll)
    def _(step):
        for i in range(unroll):
            group = step * unroll + i
            lanes = pl.ds(pl.multiple_of(group * LANES, LANES), LANES)
            values = grid_v[:, :, lanes].astype(F32).reshape(16 * 8, LANES)
            slot = group * 32 + lane // 4
            order = jnp.where(slot % 2 == 0, slot // 2, orders - 1 - slot // 2).astype(F32)
            partner = dot(values.astype(BF16), turn[...])
            forced = values + (omega_v[...] * order) * partner
            t0, t1, t2, t3 = (forced[32 * q : 32 * q + 32].astype(BF16) for q in range(4))
            a0 = jnp.where(left_half, t0, pltpu.roll(t2, 64, 1))
            a2 = jnp.where(left_half, pltpu.roll(t0, 64, 1), t2)
            a1 = jnp.where(left_half, t1, pltpu.roll(t3, 64, 1))
            a3 = jnp.where(left_half, pltpu.roll(t1, 64, 1), t3)
            packed = (
                jnp.where(first, a0, pltpu.roll(a1, 32, 1)),
                jnp.where(first, pltpu.roll(a0, 96, 1), a1),
                jnp.where(first, a2, pltpu.roll(a3, 32, 1)),
                jnp.where(first, pltpu.roll(a2, 96, 1), a3),
            )
            for d in range(4):
                near, far = packed[d][:16], packed[d][16:]
                send[0, group * 4 + d] = jnp.where(low, near, pltpu.roll(far, 4, 1)).astype(BF16)
                send[1, group * 4 + d] = jnp.where(low, pltpu.roll(near, LANES - 4, 1), far).astype(BF16)

    n = half_lats
    flip[...] = one_hot(n - 1 - iota((n, 1), 0), n)
    index = iota((256, 1), 0)
    radius = 4 * ((index // 32) % 4) + 2 * ((index // 4) % 2) + index // LANES
    spread[...] = one_hot(((index // 8) % 4) * 64 + (index % 4) * 16 + radius, 256)
    index = iota((512, 1), 0)
    for second in range(2):
        column = ((index // 16) % 4) * 64 + (index // LANES) * 16 + index % 16
        merge[second] = one_hot(jnp.where((index // 64) % 2 == second, column, -1), 256)
    index = iota((256, 1), 0)
    kind = (index // 32) % 4
    finish[...] = one_hot((2 * (index % 32) + kind % 2) * 4 + (index // LANES) * 2 + kind // 2, 256)
    spectra[...] = jnp.zeros_like(spectra)
    for u in range(4):
        out_ref[2 * u + 1, :block, :] = jnp.zeros((block, 256), BF16)

    pl.semaphore_wait(barrier, tasks - 1 + ROWS - 1)

    pltpu.make_async_copy(weights.at[:, 0], weights.at[:, 0], own_sem).wait()

    def offer(unit):
        @when(alive(unit, row))
        def _():
            for offset in (1, ROWS - 1):
                pltpu.make_async_remote_copy(
                    src_ref=weights.at[unit, row],
                    dst_ref=weights.at[unit, row],
                    send_sem=wsend_sem.at[unit],
                    recv_sem=wrecv_sem.at[offset, unit],
                    device_id={"row": lax.rem(row + offset, ROWS)},
                    device_id_type=MESH,
                ).start()

    offer(0)
    offer(1)

    def deliver(high, to):
        pltpu.make_async_remote_copy(
            src_ref=send.at[high, to],
            dst_ref=recv.at[high, task],
            send_sem=send_sem.at[high],
            recv_sem=recv_sem.at[high],
            device_id={"ta": to},
            device_id_type=MESH,
        ).start()

    planes = max(tasks // 8, 1)
    width = tasks // planes
    plane, place = task // width, task % width
    steps = sorted(range(planes), key=lambda d: -min(d, planes - d))

    for high in range(2):

        @pl.loop(0, width)
        def _(i):
            for d in steps:
                if d > 0:
                    deliver(high, lax.rem(plane + d, planes) * width + lax.rem(place + i, width))

        @pl.loop(1, width)
        def _(i):
            deliver(high, plane * width + lax.rem(place + i, width))

        if high == 0:
            offer(2)

    recv[:, task] = send[:, task]

    pltpu.make_async_copy(flat_inverses, flat_inverses, inv_sem).wait()

    def pair_inverses(start):
        @pl.loop(start // 4, (start + block) // 4)
        def _(step):
            lane = iota((1, LANES), 1)
            turned = flat_inverses[pl.ds(step * 4, 4)].reshape(LANES, LANES).T.astype(BF16)
            even = [turned[:64] if r == 0 else pltpu.roll(turned[:64], 32 * r, 1) for r in range(4)]
            odd = [turned[64:] if r == 0 else pltpu.roll(turned[64:], 32 * r, 1) for r in range(4)]
            zero = jnp.zeros_like(turned[:64])
            for i in range(4):
                top = jnp.where(lane < 32, even[-i % 4], jnp.where(lane < 64, odd[(1 - i) % 4], zero))
                bottom = jnp.where(lane < 64, zero, jnp.where(lane < 96, even[(2 - i) % 4], odd[(3 - i) % 4]))
                paired_inverses[step * 4 + i] = jnp.concatenate([top, bottom], 0)

    def relay(unit, source, to):
        @when(alive(unit, source))
        def _():
            block_ref = weights.at[unit, source]
            pltpu.make_async_copy(block_ref, block_ref, wrecv_sem.at[1 if unit == 0 else 3, unit]).wait()
            pltpu.make_async_remote_copy(
                src_ref=block_ref,
                dst_ref=block_ref,
                send_sem=wrelay_sem.at[unit],
                recv_sem=wrecv_sem.at[2, unit],
                device_id={"row": to},
                device_id_type=MESH,
            ).start()

    right, left_row, across = (lax.rem(row + i, ROWS) for i in (1, 3, 2))
    pair_inverses(0)
    relay(0, left_row, right)
    relay(1, right, left_row)
    pair_inverses(block)
    relay(2, right, left_row)

    def weights_here(unit):
        for offset, source in ((1, left_row), (2, across), (3, right)):
            if offset != 2 and (offset == 1) == (unit == 0):
                continue

            @when(alive(unit, source))
            def _():
                block_ref = weights.at[unit, source]
                pltpu.make_async_copy(block_ref, block_ref, wrecv_sem.at[offset, unit]).wait()

    def separate(high):
        rest = recv.at[high, pl.ds(0, tasks - 1)]
        pltpu.make_async_copy(rest, rest, recv_sem.at[high]).wait()
        arrived = recv[high].astype(F32)
        halves = [arrived[:, 8 * h : 8 * h + 8, :].reshape(2 * half_lats, LANES) for h in range(2)]
        northern = jnp.concatenate([half[:half_lats] for half in halves], 1)
        southern = jnp.concatenate([half[half_lats:] for half in halves], 1)
        southern = dot(flip[...], southern.astype(BF16))
        for which, part in enumerate((northern + southern, northern - southern)):
            columns = dot(part.astype(BF16), spread[...]).astype(BF16)
            for pair in range(2):
                sym_anti[high, pair, :, pl.ds(which * LANES, LANES)] = columns[:, pair * LANES : (pair + 1) * LANES]

    even_row = iota((4 * block, 1), 0) % 2 == 0
    def transform(unit):
        high = 1 if unit == 2 else 0
        for pair in range(2):
            data = sym_anti[high, pair]
            results = []
            for which in range(2):
                both = dot(weights[unit, :, 2 * pair + which].reshape(4 * block, half_lats), data)
                even_order = (which + high) % 2 == 0
                first, second = both[:, :LANES], both[:, LANES:]
                results.append(jnp.where(even_row, first, second) if even_order else jnp.where(even_row, second, first))
            merged = jnp.where(left_half, results[0], results[1]).astype(BF16)
            spec_send[unit, :, pair] = merged.reshape(4, block, LANES)
        for offset in (2, 1, 3):
            to = lax.rem(row + offset, ROWS)

            @when(alive(unit, to))
            def _():
                pltpu.make_async_remote_copy(
                    src_ref=spec_send.at[unit, to],
                    dst_ref=spec_recv.at[unit, row],
                    send_sem=ysend_sem.at[unit, offset],
                    recv_sem=yrecv_sem.at[unit, offset],
                    device_id={"row": to},
                    device_id_type=MESH,
                ).start()

        spec_recv[unit, row] = spec_send[unit, row]

    separate(0)
    weights_here(0)
    transform(0)
    weights_here(1)
    transform(1)
    separate(1)
    weights_here(2)
    transform(2)

    def arrive(unit):
        @when(alive(unit, row))
        def _():
            for offset in range(1, ROWS):
                source = lax.rem(row + ROWS - offset, ROWS)
                pltpu.make_async_copy(
                    spec_recv.at[unit, source], spec_recv.at[unit, source], yrecv_sem.at[unit, offset]
                ).wait()
            for pair in range(2):
                joined = jnp.concatenate([spec_recv[unit, r, pair] for r in range(ROWS)], 1)
                for second in range(2):
                    spectrum = dot(joined, merge[second])
                    for field in range(2):
                        spot = (2 * pair + second) * 2 + field
                        spectra[unit, pl.ds(spot, block, stride=8), :] = spectrum[:, field * LANES : (field + 1) * LANES]

    def solve(unit):
        arrive(unit)
        start = 0 if unit == 1 else block
        unroll = min(64, block)

        @pl.loop(0, block // unroll)
        def _(step):
            for i in range(unroll):
                k = step * unroll + i
                lhs = spectra[unit, pl.ds(pl.multiple_of(k * 8, 8), 8), :].astype(BF16)
                solved[unit, pl.ds(k, 8, stride=block), :] = dot(lhs, paired_inverses[start + k])

        for u in range(4):
            fields = [solved[unit, pl.ds((2 * u + field) * block, block), :] for field in range(2)]
            result = dot(jnp.concatenate(fields, 1).astype(BF16), finish[...]).astype(BF16)
            out_ref[2 * u + (1 if unit == 2 else 0), pl.ds(start, block), :] = result

    solve(0)
    solve(1)
    solve(2)

    for high in range(2):
        sent = send.at[high, pl.ds(0, tasks - 1)]
        pltpu.make_async_copy(sent, sent, send_sem.at[high]).wait()
    for unit in range(3):

        @when(alive(unit, row))
        def _():
            sent = weights.at[unit, pl.ds(0, 2)]
            pltpu.make_async_copy(sent, sent, wsend_sem.at[unit]).wait()

        @when(alive(unit, left_row if unit == 0 else right))
        def _():
            sent = weights.at[unit, 0]
            pltpu.make_async_copy(sent, sent, wrelay_sem.at[unit]).wait()

        for offset in range(1, ROWS):
            to = lax.rem(row + offset, ROWS)

            @when(alive(unit, to))
            def _():
                sent = spec_send.at[unit, to]
                pltpu.make_async_copy(sent, sent, ysend_sem.at[unit, offset]).wait()


def shards(tasks, grid, omega, legendre_weights, radial_inverses):
    block = tasks
    half_lats = 4 * tasks
    in_hbm = pl.BlockSpec(memory_space=pltpu.HBM)
    in_vmem = pl.BlockSpec(memory_space=pltpu.VMEM)
    dma = pltpu.SemaphoreType.DMA
    return pl.pallas_call(
        functools.partial(kernel, tasks),
        out_shape=jax.ShapeDtypeStruct(legendre_weights.shape[:2] + (256,), BF16),
        in_specs=[in_hbm] * 4,
        out_specs=in_vmem,
        scratch_shapes=[
            pltpu.VMEM((LANES, LANES), BF16),
            pltpu.VMEM((16, 8, 32 * tasks), BF16),
            pltpu.VMEM((8, 16), F32),
            pltpu.VMEM((128, LANES), F32),
            pltpu.VMEM((2, tasks, 16, LANES), BF16),
            pltpu.VMEM((2, tasks, 16, LANES), BF16),
            pltpu.VMEM((3, ROWS, 4, block, half_lats), BF16),
            pltpu.VMEM((2 * block, 32, LANES), F32),
            pltpu.VMEM((2 * block, LANES, LANES), BF16),
            pltpu.VMEM((half_lats, half_lats), BF16),
            pltpu.VMEM((256, 256), BF16),
            pltpu.VMEM((2, 2, half_lats, 256), BF16),
            pltpu.VMEM((3, ROWS, 2, block, LANES), BF16),
            pltpu.VMEM((3, ROWS, 2, block, LANES), BF16),
            pltpu.VMEM((2, 512, 256), BF16),
            pltpu.VMEM((3, block * 8 + 8, LANES), F32),
            pltpu.VMEM((3, block * 9, LANES), F32),
            pltpu.VMEM((256, 256), BF16),
            dma, dma, dma, dma, dma((2,)), dma((2,)),
            dma((3,)), dma((ROWS, 3)), dma((3,)), dma((3, ROWS)), dma((3, ROWS)),
        ],
        compiler_params=pltpu.CompilerParams(
            collective_id=0, has_side_effects=True, vmem_limit_bytes=60 * 1024 * 1024
        ),
    )(grid, omega.T, legendre_weights, radial_inverses)


def solution(mesh):
    in_specs = (P("row", "ta", None), P("row", "ta"), P("ta", "row", None), P("row", None))
    out_specs = P("ta", "row", None)
    return jax.shard_map(
        functools.partial(shards, mesh.shape["ta"]), mesh=mesh, in_specs=in_specs, out_specs=out_specs, check_vma=False
    )
```
